32 devices in a mesh: fsdp: 8 (over z, x), ctx: 2 (over y), tp: 2 (over core).
Axes of the slice: x: 2, y: 2, z: 4, core: 2. Of those that a mesh axis runs over, the one named last changes fastest.
Arguments:
- latents_in: float32 [32, 1024, 384], P('fsdp', 'ctx'), may hold values from -6 to 6
- condition: float32 [32, 384], P('fsdp'), may hold values from -6 to 6
- w_mod: bfloat16 [384, 6, 384], P('fsdp', 'tp'), may hold values from -0.3125 to 0.3125
- b_mod: bfloat16 [6, 384], P('tp', 'fsdp'), may hold values from -3 to 3
- w_qkv: bfloat16 [384, 3, 384], P('fsdp', None, 'tp'), may hold values from -0.3125 to 0.3125
- b_qv: bfloat16 [2, 384], P(None, ('tp', 'fsdp')), may hold values from -3 to 3
- w_out: bfloat16 [384, 384], P('tp', 'fsdp'), may hold values from -3 to 3
- b_out: bfloat16 [384], P('fsdp'), may hold values from -3 to 3
- up_weight: bfloat16 [384, 1536], P('fsdp', 'tp'), may hold values from -0.3125 to 0.3125
- up_projection_bias: bfloat16 [1536], P(('tp', 'fsdp')), may hold values from -3 to 3
- down_weight: bfloat16 [1536, 384], P('tp', 'fsdp'), may hold values from -0.15625 to 0.15625
- down_projection_bias: bfloat16 [384], P('fsdp'), may hold values from -3 to 3
- cotangent: float32 [32, 1024, 384], P('fsdp', 'ctx'), may hold values from -6 to 6
Outputs:
- block_out: float32 [32, 1024, 384], P('fsdp', 'ctx')
- latents_grad: float32 [32, 1024, 384], P('fsdp', 'ctx')
- condition_grad: float32 [32, 384], P('fsdp')
- w_mod_grad: float32 [384, 6, 384], P('fsdp', 'tp')
- b_mod_grad: float32 [6, 384], P('tp', 'fsdp')
- w_qkv_grad: float32 [384, 3, 384], P('fsdp', None, 'tp')
- b_qv_grad: float32 [2, 384], P(None, ('tp', 'fsdp'))
- w_out_grad: float32 [384, 384], P('tp', 'fsdp')
- b_out_grad: float32 [384], P('fsdp')
- w_up_grad: float32 [384, 1536], P('fsdp', 'tp')
- b_up_grad: float32 [1536], P(('tp', 'fsdp'))
- w_down_grad: float32 [1536, 384], P('tp', 'fsdp')
- b_down_grad: float32 [384], P('fsdp')
The draws below stay inside these ranges and needn't reach their ends.
All inputs are finite; a program needn't handle non-finite values.
Results may differ from the reference program's by a relative error of at most 0.013.
The reference program's roundings to bfloat16 on the way count: a program that leaves them out, or rounds other values in their place, can miss the bound.
Values may be sent and summed in bfloat16 or wider, within the bound.
A program may use at most 128 MiB of HBM per device.

```python
import math
import jax
import jax.numpy as jnp
from jax import lax

D = 384
H = 6
HD = 64
FF = 1536
SEQ = 1024
LATENTS = 32


def steps_of(own_key, dims, split, least, high):
    gain = 1.0
    for axis_at, shards_of in split:
        heights = jax.random.uniform(jax.random.fold_in(jax.random.fold_in(own_key, 6), axis_at), (shards_of,), jnp.float32, least / len(split), high / len(split))
        gain = gain * jnp.repeat(jnp.exp(heights), dims[axis_at] // shards_of).reshape((-1,) + (1,) * (len(dims) - 1 - axis_at))
    return gain


def noise(own_key, shape, width, reach, cuts=(), held_as=jnp.bfloat16):
    entries = jax.random.normal(own_key, shape, jnp.float32) * width
    if len(cuts) > 0:
        entries = steps_of(own_key, shape, cuts, -0.22, 0.18) * entries
    return jnp.clip(entries, min=-reach, max=reach).astype(held_as)


def setup_inputs(seed: int = 0) -> dict:
    keys = jax.random.split(jax.random.key(seed), 14)
    latents_in = noise(keys[0], (LATENTS, SEQ, D), 1.0, 6.0, ((0, 8), (1, 2)), jnp.float32)
    condition = noise(keys[1], (LATENTS, D), 1.0, 6.0, ((0, 8),), jnp.float32)
    w_mod = noise(keys[2], (D, 6, D), D ** -0.5, 0.3125, ((0, 8), (1, 2)))
    b_mod = noise(keys[3], (6, D), 0.5, 3.0, ((0, 2), (1, 8)))
    w_qkv = noise(keys[4], (D, 3, D), D ** -0.5, 0.3125, ((0, 8), (2, 2)))
    b_qv = noise(keys[5], (2, D), 0.5, 3.0, ((1, 16),))
    w_out = noise(keys[6], (D, D), 0.6, 3.0, ((0, 2), (1, 8)))
    b_out = noise(keys[7], (D,), 0.5, 3.0, ((0, 8),))
    up_weight = noise(keys[8], (D, FF), D ** -0.5, 0.3125, ((0, 8), (1, 2)))
    up_projection_bias = noise(keys[9], (FF,), 0.5, 3.0, ((0, 16),))
    down_weight = noise(keys[10], (FF, D), FF ** -0.5, 0.15625, ((0, 2), (1, 8)))
    down_projection_bias = noise(keys[11], (D,), 0.5, 3.0, ((0, 8),))
    cotangent = noise(keys[12], (LATENTS, SEQ, D), 1.0, 6.0, ((0, 8), (1, 2)), jnp.float32)
    return dict(latents_in=latents_in, condition=condition, w_mod=w_mod, b_mod=b_mod, w_qkv=w_qkv, b_qv=b_qv, w_out=w_out, b_out=b_out, up_weight=up_weight, up_projection_bias=up_projection_bias, down_weight=down_weight, down_projection_bias=down_projection_bias, cotangent=cotangent)


@jax.custom_vjp
def low(v):
    return lax.optimization_barrier(v.astype(jnp.bfloat16)).astype(jnp.float32)

@jax.custom_vjp
def reduced_precision_backward(v):
    return v

def low_keep(v):
    return (low(v), None)

def low_pass(kept, grad):
    return (grad,)

def back_keep(v):
    return (v, None)

def back_low(kept, grad):
    return (low(grad),)
low.defvjp(low_keep, low_pass)
reduced_precision_backward.defvjp(back_keep, back_low)
TOP_PRECISION = lax.Precision.HIGHEST

def normalize(values):
    centre = values - lax.optimization_barrier(jnp.mean(values, axis=-1, keepdims=True))
    return centre * lax.rsqrt(lax.optimization_barrier(jnp.mean(centre * centre, axis=-1, keepdims=True)) + 1e-06)

def attend(blocks):
    query_rows, key_rows, value_rows = blocks
    length = query_rows.shape[0]
    queries = query_rows.reshape(length, H, HD)
    keys_here = key_rows.reshape(length, H, HD)
    values_here = value_rows.reshape(length, H, HD)
    scores = reduced_precision_backward(jnp.einsum('qhc,khc->hqk', queries, keys_here, precision=TOP_PRECISION) * (1.0 / math.sqrt(HD)))
    softmax_rows = jax.nn.softmax(scores, axis=-1)
    mixed_rows = jnp.einsum('hqk,khc->qhc', low(softmax_rows), values_here, precision=TOP_PRECISION)
    return mixed_rows.reshape(length, H * HD)

def forward(latents_in, condition, w_mod, b_mod, w_qkv, b_qv, w_out, b_out, up_weight, up_projection_bias, down_weight, down_projection_bias):
    silu_cond = low(jax.nn.silu(condition))
    modulation = jnp.einsum('ld,dkc->lkc', silu_cond, w_mod, precision=TOP_PRECISION) + b_mod
    stretches = [modulation[:, stretch_index][:, None, :] for stretch_index in range(6)]
    shift_one, scale_one, gate_one, shift_two, scale_two, gate_two = stretches
    hidden_one = low(normalize(latents_in) * (1.0 + scale_one) + shift_one)
    projected = jnp.einsum('lsd,dkc->lskc', hidden_one, w_qkv, precision=TOP_PRECISION)
    query_rows = low(reduced_precision_backward(projected[:, :, 0] + b_qv[0]))
    key_rows = low(reduced_precision_backward(projected[:, :, 1]))
    value_rows = low(reduced_precision_backward(projected[:, :, 2] + b_qv[1]))
    attended = lax.map(jax.checkpoint(attend), (query_rows, key_rows, value_rows))
    attended = low(reduced_precision_backward(attended))
    branch = reduced_precision_backward(jnp.einsum('lsc,cd->lsd', attended, w_out, precision=TOP_PRECISION) + b_out)
    middle = latents_in + gate_one * branch
    second_hidden_state = low(normalize(middle) * (1.0 + scale_two) + shift_two)
    up_projection_input = reduced_precision_backward(jnp.einsum('vae,et->vat', second_hidden_state, up_weight, precision=TOP_PRECISION) + up_projection_bias)
    activation_value = low(jax.nn.gelu(up_projection_input, approximate=True))
    feedforward_output = reduced_precision_backward(jnp.einsum('vmr,rh->vmh', activation_value, down_weight, precision=TOP_PRECISION) + down_projection_bias)
    return middle + gate_two * feedforward_output

def reference(latents_in, condition, w_mod, b_mod, w_qkv, b_qv, w_out, b_out, up_weight, up_projection_bias, down_weight, down_projection_bias, cotangent):
    block_out, pullback = jax.vjp(forward, latents_in, condition, w_mod.astype(jnp.float32), b_mod.astype(jnp.float32), w_qkv.astype(jnp.float32), b_qv.astype(jnp.float32), w_out.astype(jnp.float32), b_out.astype(jnp.float32), up_weight.astype(jnp.float32), up_projection_bias.astype(jnp.float32), down_weight.astype(jnp.float32), down_projection_bias.astype(jnp.float32))
    grads = pullback(cotangent)
    return (block_out, grads[0], grads[1], grads[2], grads[3], grads[4], grads[5], grads[6], grads[7], grads[8], grads[9], grads[10], grads[11])
```

```python
import functools
import math

import jax
import jax.numpy as jnp
from jax import lax
from jax.experimental import pallas as pl
from jax.experimental.pallas import tpu as pltpu
from jax.sharding import PartitionSpec as P

HD = 64
EPSILON = 1e-06
MESH = pl.DeviceIdType.MESH


def normalize(values):
    centre = values - jnp.mean(values, axis=-1, keepdims=True)
    inverse = lax.rsqrt(jnp.mean(centre * centre, axis=-1, keepdims=True) + EPSILON)
    return (centre * inverse, inverse)


def norm_back(upstream, normed, inverse):
    return inverse * (
        upstream
        - jnp.mean(upstream, axis=-1, keepdims=True)
        - normed * jnp.mean(upstream * normed, axis=-1, keepdims=True)
    )


def remote(src, dst, send, recv, device):
    return pltpu.make_async_remote_copy(
        src_ref=src, dst_ref=dst, send_sem=send, recv_sem=recv,
        device_id=device, device_id_type=MESH,
    )


def greet(F, f, c, t):
    barrier = pltpu.get_barrier_semaphore()
    pl.semaphore_signal(barrier, inc=1, device_id={"tp": 1 - t}, device_id_type=MESH)
    pl.semaphore_signal(barrier, inc=1, device_id={"ctx": 1 - c}, device_id_type=MESH)

    def one(k, carry):
        pl.semaphore_signal(
            barrier, inc=1, device_id={"fsdp": lax.rem(f + k, F)}, device_id_type=MESH
        )
        return carry

    lax.fori_loop(1, F, one, 0)
    pl.semaphore_wait(barrier, F + 1)


def each_peer(F, f, body):
    def one(k, carry):
        body(k, lax.rem(f + k, F), lax.rem(f + F - k, F))
        return carry

    lax.fori_loop(1, F, one, 0)


def gather_kernel(
    F, C, T,
    w_ref, x_ref, ct_ref, sc_ref, bs_ref, wm_ref,
    W, X, CT, SC, BS, MO,
    MP, MR,
    w_s, w_r, wt_s, wt_r, sc_s, sc_r, bs_s, bs_r, m_s, m_r, big_s, big_r, loc,
):
    f, c, t = lax.axis_index("fsdp"), lax.axis_index("ctx"), lax.axis_index("tp")
    greet(F, f, c, t)
    other_core, other_half = {"tp": 1 - t}, {"ctx": 1 - c}

    def sc_copy(k, to, at):
        return remote(sc_ref, SC.at[at], sc_s.at[k], sc_r.at[at], {"fsdp": to})

    def bs_copy(k, to, at):
        return remote(bs_ref, BS.at[t, at], bs_s.at[k], bs_r.at[at], {"fsdp": to})

    def w_copy(k, to, at):
        return remote(w_ref, W.at[t, at], w_s.at[k], w_r.at[at], {"fsdp": to})

    def m_copy(k, to, at):
        return remote(MP.at[to], MR.at[at], m_s.at[k], m_r.at[at], {"fsdp": to})

    def core_copy(at):
        return remote(W.at[t, at], W.at[t, at], wt_s.at[at], wt_r.at[at], other_core)

    own_first = remote(w_ref, W.at[t, f], wt_s.at[f], wt_r.at[f], other_core)
    send_x = remote(x_ref.at[T * (1 - c) + t], X.at[c], big_s.at[0], big_r.at[0], other_half)
    send_ct = remote(ct_ref.at[T * (1 - c) + t], CT.at[c], big_s.at[1], big_r.at[1], other_half)
    keep_x = pltpu.make_async_copy(x_ref.at[T * c + t], X.at[c], loc.at[0])
    keep_ct = pltpu.make_async_copy(ct_ref.at[T * c + t], CT.at[c], loc.at[1])
    keep_w = pltpu.make_async_copy(w_ref, W.at[t, f], loc.at[2])

    def start_small(k, to, source):
        sc_copy(k, to, f).start()
        bs_copy(k, to, f).start()

    each_peer(F, f, start_small)
    each_peer(F, f, lambda k, to, source: w_copy(k, to, f).start())
    send_x.start()
    send_ct.start()
    own_first.start()
    keep_x.start()
    keep_ct.start()
    keep_w.start()
    SC[f] = sc_ref[...]
    BS[t, f] = bs_ref[...]
    each_peer(F, f, lambda k, to, source: sc_copy(k, to, source).wait_recv())
    rows = SC[...].reshape(F * SC.shape[1], SC.shape[2]).astype(jnp.bfloat16)
    MP[...] = jnp.dot(rows, wm_ref[...], preferred_element_type=jnp.float32).reshape(MP.shape)
    each_peer(F, f, lambda k, to, source: m_copy(k, to, f).start())
    MR[f] = MP[f]
    each_peer(F, f, lambda k, to, source: bs_copy(k, to, source).wait_recv())
    send_bs = remote(BS.at[t], BS.at[t], big_s.at[2], big_r.at[2], other_core)
    send_bs.start()
    each_peer(F, f, lambda k, to, source: m_copy(k, to, source).wait_recv())
    MO[t] = jnp.sum(MR[...], axis=0)
    send_mo = remote(MO.at[t], MO.at[t], big_s.at[3], big_r.at[3], other_core)
    send_mo.start()

    def forward(k, to, source):
        w_copy(k, to, source).wait_recv()
        core_copy(source).start()

    each_peer(F, f, forward)

    def finish(k, to, source):
        sc_copy(k, to, f).wait_send()
        bs_copy(k, to, f).wait_send()
        w_copy(k, to, f).wait_send()
        m_copy(k, to, f).wait_send()
        core_copy(source).wait()

    each_peer(F, f, finish)
    own_first.wait()
    send_x.wait()
    send_ct.wait()
    send_bs.wait()
    send_mo.wait()
    keep_x.wait()
    keep_ct.wait()
    keep_w.wait()


def gather(mesh, packed, latents, cotangent, cond_rows, biases, mod_weight):
    F, C, T = mesh.shape["fsdp"], mesh.shape["ctx"], mesh.shape["tp"]
    half, width = latents.shape[1:]
    rows, columns = cond_rows.shape[0], mod_weight.shape[1]
    anywhere = pl.BlockSpec(memory_space=pl.ANY)
    vmem = pl.BlockSpec(memory_space=pltpu.VMEM)
    dma = pltpu.SemaphoreType.DMA
    return pl.pallas_call(
        functools.partial(gather_kernel, F, C, T),
        out_shape=(
            jax.ShapeDtypeStruct((T, F) + packed.shape, packed.dtype),
            jax.ShapeDtypeStruct((C, half, width), jnp.float32),
            jax.ShapeDtypeStruct((C, half, width), jnp.float32),
            jax.ShapeDtypeStruct((F, rows, width), jnp.float32),
            jax.ShapeDtypeStruct((T, F) + biases.shape, jnp.float32),
            jax.ShapeDtypeStruct((T, rows, columns), jnp.float32),
        ),
        in_specs=[anywhere, anywhere, anywhere, vmem, vmem, vmem],
        out_specs=(anywhere, anywhere, anywhere, vmem, vmem, vmem),
        scratch_shapes=[
            pltpu.VMEM((F, rows, columns), jnp.float32),
            pltpu.VMEM((F, rows, columns), jnp.float32),
        ] + [dma((F,))] * 10 + [dma((4,)), dma((4,)), dma((3,))],
        compiler_params=pltpu.CompilerParams(
            collective_id=0, has_side_effects=True, vmem_limit_bytes=40 << 20
        ),
        name="gather",
    )(packed, latents, cotangent, cond_rows, biases, mod_weight)


def reduce_kernel(
    F, C, T,
    gp, lg, mg_ref, wm_ref,
    GO, LO, MG, CO,
    A, S1, B, S2, R, CP, CR, CX,
    a_s, a_r, b_s, b_r, r_s, r_r, mg_s, mg_r, c_s, c_r, big_s, big_r, loc,
):
    f, c, t = lax.axis_index("fsdp"), lax.axis_index("ctx"), lax.axis_index("tp")
    deep = wm_ref.shape[1]
    greet(F, f, c, t)
    other_core, other_half = {"tp": 1 - t}, {"ctx": 1 - c}

    def mg_copy(k, to, at):
        return remote(mg_ref, MG.at[c, t, at], mg_s.at[k], mg_r.at[at], {"fsdp": to})

    def a_copy(h, at):
        return remote(gp.at[1 - t, h, at], A.at[h, at], a_s.at[h, at], a_r.at[h, at], other_core)

    def b_copy(at):
        return remote(S1.at[1 - c, at], B.at[at], b_s.at[at], b_r.at[at], other_half)

    def r_copy(to, at):
        return remote(S2.at[to], R.at[at], r_s.at[to], r_r.at[at], {"fsdp": to})

    def c_copy(to, at):
        return remote(CP.at[to], CR.at[at], c_s.at[to], c_r.at[at], {"fsdp": to})

    def over_blocks(body):
        def one(k, carry):
            body(lax.rem(f + k, F))
            return carry

        lax.fori_loop(1, F + 1, one, 0)

    each_peer(F, f, lambda k, to, source: mg_copy(k, to, f).start())

    def start_a(at):
        a_copy(1 - c, at).start()
        a_copy(c, at).start()

    over_blocks(start_a)
    own = T * c + t
    keep = pltpu.make_async_copy(lg.at[c], LO.at[own], loc)
    keep.start()
    MG[c, t, f] = mg_ref[...]

    def add(one, two):
        return (one.astype(jnp.float32) + two.astype(jnp.float32)).astype(jnp.bfloat16)

    def first(at):
        for away, h in enumerate((c, 1 - c)[::-1]):
            a_copy(h, at).wait_recv()
            S1[h, at] = add(gp[t, h, at], A[h, at])
            if away == 0:
                b_copy(at).start()

    over_blocks(first)
    send_lg = remote(lg.at[1 - c], LO.at[own], big_s.at[0], big_r.at[0], other_half)
    send_lg.start()
    each_peer(F, f, lambda k, to, source: mg_copy(k, to, source).wait_recv())
    mg_core = remote(MG.at[c, t], MG.at[c, t], big_s.at[1], big_r.at[1], other_core)
    mg_core.start()

    def second(at):
        b_copy(at).wait_recv()
        S2[at] = add(S1[c, at], B[at])

    def second_peer(k, to, source):
        second(to)
        r_copy(to, f).start()

    mg_core.wait()
    mg_half = remote(MG.at[c], MG.at[c], big_s.at[2], big_r.at[2], other_half)
    mg_half.start()
    each_peer(F, f, second_peer)
    second(f)
    mg_half.wait()
    CP[...] = jnp.zeros_like(CP)
    for c2 in range(C):
        for t2 in range(T):
            total = jnp.zeros((F, deep), jnp.float32)
            for k in range(3):
                row = jnp.where(t == 0, MG[c2, t2, :, k, :], MG[c2, t2, :, 3 + k, :])
                total += lax.dot_general(
                    row, wm_ref[k].astype(jnp.float32), (((1,), (1,)), ((), ())),
                    precision=lax.Precision.HIGHEST, preferred_element_type=jnp.float32,
                )
            CP[:, T * c2 + t2, 0:deep] = total
    each_peer(F, f, lambda k, to, source: c_copy(to, f).start())
    CR[f] = CP[f]
    send_lg.wait_recv()
    keep.wait()

    def core_lg(n, at):
        return remote(LO.at[at], LO.at[at], big_s.at[3 + n], big_r.at[3 + n], other_core)

    core_lg(0, own).start()
    core_lg(1, T * (1 - c) + t).start()
    R[f] = S2[f]
    each_peer(F, f, lambda k, to, source: r_copy(to, source).wait_recv())
    total = lax.fori_loop(
        0, F, lambda k, sum_: sum_ + R[k].astype(jnp.float32),
        jnp.zeros(R.shape[1:], jnp.float32),
    )
    GO[c] = total.astype(jnp.bfloat16)
    go_half = remote(GO.at[c], GO.at[c], big_s.at[5], big_r.at[5], other_half)
    go_half.start()
    each_peer(F, f, lambda k, to, source: c_copy(to, source).wait_recv())
    c_core = remote(CR, CX, big_s.at[6], big_r.at[6], other_core)
    c_core.start()
    c_core.wait()
    CO[...] = CR[...] + CX[...]

    def finish(k, to, source):
        mg_copy(k, to, f).wait_send()
        r_copy(to, f).wait_send()
        c_copy(to, f).wait_send()

    each_peer(F, f, finish)

    def finish_block(at):
        a_copy(1 - c, at).wait_send()
        a_copy(c, at).wait_send()
        b_copy(at).wait_send()

    over_blocks(finish_block)
    send_lg.wait_send()
    go_half.wait()
    core_lg(0, own).wait()
    core_lg(1, T * (1 - c) + t).wait()


def reduce(mesh, grads, latents_grad, mod_grad, mod_weight):
    F, C, T = mesh.shape["fsdp"], mesh.shape["ctx"], mesh.shape["tp"]
    half, width = latents_grad.shape[1:]
    block = grads.shape[3:]
    anywhere = pl.BlockSpec(memory_space=pl.ANY)
    vmem = pl.BlockSpec(memory_space=pltpu.VMEM)
    dma = pltpu.SemaphoreType.DMA
    low = jnp.bfloat16
    return pl.pallas_call(
        functools.partial(reduce_kernel, F, C, T),
        out_shape=(
            jax.ShapeDtypeStruct((C,) + block, low),
            jax.ShapeDtypeStruct((C * T, half, width), jnp.float32),
            jax.ShapeDtypeStruct((C, T, F) + mod_grad.shape, jnp.float32),
            jax.ShapeDtypeStruct((F, 8, 128), jnp.float32),
        ),
        in_specs=[vmem, anywhere, vmem, vmem],
        out_specs=(vmem, anywhere, vmem, vmem),
        scratch_shapes=[
            pltpu.VMEM((C, F) + block, low),
            pltpu.VMEM((C, F) + block, low),
            pltpu.VMEM((F,) + block, low),
            pltpu.VMEM((F,) + block, low),
            pltpu.VMEM((F,) + block, low),
            pltpu.VMEM((F, 8, 128), jnp.float32),
            pltpu.VMEM((F, 8, 128), jnp.float32),
            pltpu.VMEM((F, 8, 128), jnp.float32),
            dma((C, F)), dma((C, F)),
        ] + [dma((F,))] * 8 + [dma((7,)), dma((7,)), dma],
        compiler_params=pltpu.CompilerParams(
            collective_id=1, has_side_effects=True, vmem_limit_bytes=56 << 20
        ),
        name="reduce",
    )(grads, latents_grad, mod_grad, mod_weight)


def attend_forward(blocks):
    query_rows, key_rows, value_rows = blocks
    scores = jnp.einsum(
        "qc,kc->qk", query_rows, key_rows, preferred_element_type=jnp.float32
    ) * (1.0 / math.sqrt(HD))
    highest = jnp.max(scores, axis=-1, keepdims=True)
    exponent = jnp.exp(scores - highest)
    totals = jnp.sum(exponent, axis=-1, keepdims=True)
    softmax_rows = (exponent / totals).astype(jnp.bfloat16)
    mixed_rows = jnp.dot(softmax_rows, value_rows, preferred_element_type=jnp.float32)
    return (mixed_rows.astype(jnp.bfloat16), highest + jnp.log(totals))


def attend_backward(blocks):
    query_rows, key_rows, value_rows, attended_grad, log_totals = blocks
    factor = 1.0 / math.sqrt(HD)
    scores = (
        jnp.einsum("qc,kc->qk", query_rows, key_rows, preferred_element_type=jnp.float32) * factor
    )
    softmax_rows = jnp.exp(scores - log_totals)
    prob_grad = jnp.einsum(
        "qc,kc->qk", attended_grad, value_rows, preferred_element_type=jnp.float32
    )
    row_inner = jnp.sum(prob_grad * softmax_rows, axis=-1, keepdims=True)
    score_grad = (softmax_rows * (prob_grad - row_inner)).astype(jnp.bfloat16)
    query_grad = jnp.dot(score_grad, key_rows, preferred_element_type=jnp.float32) * factor
    key_grad = (
        jnp.einsum("qk,qc->kc", score_grad, query_rows, preferred_element_type=jnp.float32) * factor
    )
    value_grad = jnp.einsum(
        "qk,qc->kc",
        softmax_rows.astype(jnp.bfloat16),
        attended_grad,
        preferred_element_type=jnp.float32,
    )
    low = jnp.bfloat16
    return (query_grad.astype(low), key_grad.astype(low), value_grad.astype(low))


def attention(queries, keys, values):
    return lax.map(attend_forward, (queries, keys, values))


def attention_back(queries, keys, values, attended_grad, log_totals):
    return lax.map(attend_backward, (queries, keys, values, attended_grad, log_totals))


def split_heads(rows):
    return rows.reshape(rows.shape[0], rows.shape[1] // HD, HD).transpose(1, 0, 2)


def join_heads(heads):
    return heads.transpose(1, 0, 2).reshape(heads.shape[1], heads.shape[0] * heads.shape[2])


def dot(a, b):
    return jnp.dot(a, b, preferred_element_type=jnp.float32)


def dot_bt(a, b):
    return lax.dot_general(a, b, (((1,), (1,)), ((), ())), preferred_element_type=jnp.float32)


def dot_at(a, b):
    return lax.dot_general(a, b, (((0,), (0,)), ((), ())), preferred_element_type=jnp.float32)


def shards(
    mesh,
    latents_in,
    condition,
    w_mod,
    b_mod,
    w_qkv,
    b_qv,
    w_out,
    b_out,
    up_weight,
    up_projection_bias,
    down_weight,
    down_projection_bias,
    cotangent,
):
    F, C, T = mesh.shape["fsdp"], mesh.shape["ctx"], mesh.shape["tp"]
    f, c, t = lax.axis_index("fsdp"), lax.axis_index("ctx"), lax.axis_index("tp")
    group, half, width = latents_in.shape
    assert C == 2 and T == 2 and group == C * T
    deep = w_mod.shape[0]
    part = w_qkv.shape[2]
    hidden = up_weight.shape[1]
    low = jnp.bfloat16
    full = jnp.float32
    own = T * c + t

    packed = jnp.concatenate(
        [w_qkv.reshape(deep, 3 * part), w_out.T, up_weight, down_weight.T], axis=1
    )
    columns = packed.shape[1]
    flat_bias = jnp.concatenate(
        [
            b_mod.reshape(-1), b_qv.reshape(-1), b_out, up_projection_bias, down_projection_bias,
        ]
    ).astype(full)
    bias_rows = -(-flat_bias.shape[0] // 1024) * 8
    biases = jnp.pad(flat_bias, (0, bias_rows * 128 - flat_bias.shape[0])).reshape(bias_rows, 128)
    silu_cond = jax.nn.silu(condition).astype(low)
    cond_rows = jnp.pad(silu_cond.astype(full), ((0, 8 - group), (0, 0)))
    mod_padded = lax.dynamic_update_slice(
        jnp.zeros((width, 3 * width), low), w_mod.reshape(deep, 3 * width), (f * deep, 0)
    )
    weights, x, cot, cond_all, bias_all, mod_all = gather(
        mesh, packed, latents_in, cotangent, cond_rows, biases, mod_padded
    )
    x = x.reshape(C * half, width)
    cot = cot.reshape(C * half, width)
    weights = weights.reshape(T, width, columns)

    def cut(tensor, start, size):
        return tensor[:, :, start : start + size]

    qkv_full = (
        cut(weights, 0, 3 * part).reshape(T, width, 3, part).transpose(1, 2, 0, 3)
        .reshape(width, 3 * width)
    )
    outs_t = cut(weights, 3 * part, part).transpose(1, 0, 2).reshape(width, width)
    up_full = cut(weights, 4 * part, hidden).transpose(1, 0, 2).reshape(width, T * hidden)
    down_t = cut(weights, 4 * part + hidden, hidden).transpose(1, 0, 2).reshape(width, T * hidden)

    bias_all = bias_all.reshape(T, F, -1)
    edges = [3 * deep, b_qv.size, b_out.size, up_projection_bias.size, down_projection_bias.size]
    pieces, start = [], 0
    for size in edges:
        pieces.append(bias_all[:, :, start : start + size])
        start += size
    mod_bias = pieces[0].reshape(T, F, 3, deep).transpose(0, 2, 1, 3).reshape(6, width)
    qv_bias = pieces[1].reshape(T, F, 2, -1).transpose(2, 0, 1, 3).reshape(2, width)
    out_bias = pieces[2][0].reshape(width)
    up_bias = pieces[3].reshape(T * hidden)
    down_bias = pieces[4][0].reshape(width)

    modulation = lax.dynamic_index_in_dim(mod_all, own, 1, keepdims=False)
    modulation = modulation.reshape(6, width) + mod_bias
    shift_one, scale_one, gate_one, shift_two, scale_two, gate_two = (
        modulation[k : k + 1] for k in range(6)
    )

    normed_one, inverse_one = normalize(x)
    hidden_one = (normed_one * (1.0 + scale_one) + shift_one).astype(low)
    projected = dot(hidden_one, qkv_full)
    queries = split_heads((projected[:, :width] + qv_bias[0]).astype(low))
    keys = split_heads(projected[:, width : 2 * width].astype(low))
    values = split_heads((projected[:, 2 * width :] + qv_bias[1]).astype(low))
    attended_heads, log_totals = attention(queries, keys, values)
    attended = join_heads(attended_heads)
    branch = dot_bt(attended, outs_t) + out_bias
    middle = x + gate_one * branch
    normed_two, inverse_two = normalize(middle)
    hidden_two = (normed_two * (1.0 + scale_two) + shift_two).astype(low)
    upper_in = dot(hidden_two, up_full) + up_bias
    gelu_value, gelu_pull = jax.vjp(lambda u: jax.nn.gelu(u, approximate=True), upper_in)
    active = gelu_value.astype(low)
    mlp_out = dot_bt(active, down_t) + down_bias
    block_own = (middle + gate_two * mlp_out).reshape(C, half, width)

    away = lax.dynamic_index_in_dim(block_own, 1 - c, 0, keepdims=False)
    here = lax.dynamic_index_in_dim(block_own, c, 0, keepdims=False)
    landed = lax.ppermute(away, "ctx", [(0, 1), (1, 0)])
    pair = jnp.where(c == 0, jnp.stack([here, landed]), jnp.stack([landed, here]))
    other_pair = lax.ppermute(pair, "tp", [(0, 1), (1, 0)])
    block_out = jnp.where(
        t == 0, jnp.stack([pair, other_pair], 1), jnp.stack([other_pair, pair], 1)
    ).reshape(group, half, width)

    gate_two_grad = jnp.sum(cot * mlp_out, axis=0)
    down_in = (cot * gate_two).astype(low)
    down_bias_grad = jnp.sum(down_in, axis=0, dtype=full)
    down_grad_t = dot_at(down_in, active)
    upper_grad = gelu_pull(dot(down_in, down_t))[0].astype(low)
    up_bias_grad = jnp.sum(upper_grad, axis=0, dtype=full)
    up_grad = dot_at(hidden_two, upper_grad)
    hidden_two_grad = dot_bt(upper_grad, up_full)
    scale_two_grad = jnp.sum(hidden_two_grad * normed_two, axis=0)
    shift_two_grad = jnp.sum(hidden_two_grad, axis=0)
    middle_grad = cot + norm_back(hidden_two_grad * (1.0 + scale_two), normed_two, inverse_two)
    gate_one_grad = jnp.sum(middle_grad * branch, axis=0)
    branch_grad = (middle_grad * gate_one).astype(low)
    out_bias_grad = jnp.sum(branch_grad, axis=0, dtype=full)
    out_grad_t = dot_at(branch_grad, attended)
    attended_grad = split_heads(dot(branch_grad, outs_t).astype(low))
    query_grad, key_grad, value_grad = attention_back(
        queries, keys, values, attended_grad, log_totals
    )
    projected_grad = jnp.concatenate(
        [join_heads(query_grad), join_heads(key_grad), join_heads(value_grad)], axis=1
    )
    all_bias_grad = jnp.sum(projected_grad, axis=0, dtype=full)
    qkv_grad = dot_at(hidden_one, projected_grad)
    hidden_one_grad = dot_bt(projected_grad, qkv_full)
    scale_one_grad = jnp.sum(hidden_one_grad * normed_one, axis=0)
    shift_one_grad = jnp.sum(hidden_one_grad, axis=0)
    latents_grad = middle_grad + norm_back(
        hidden_one_grad * (1.0 + scale_one), normed_one, inverse_one
    )
    zeros = jnp.zeros((width,), full)
    mod_grad = jnp.stack(
        [
            shift_one_grad, scale_one_grad, gate_one_grad,
            shift_two_grad, scale_two_grad, gate_two_grad, zeros, zeros,
        ]
    )

    def by_owner(grad, size):
        return grad.astype(low).reshape(F, deep, T, size).transpose(2, 0, 1, 3)

    grads = jnp.concatenate(
        [
            qkv_grad.astype(low).reshape(F, deep, 3, T, part).transpose(3, 0, 1, 2, 4)
            .reshape(T, F, deep, 3 * part),
            by_owner(out_grad_t, part),
            by_owner(up_grad, hidden),
            by_owner(down_grad_t, hidden),
        ],
        axis=3,
    )
    grads = grads.reshape(T, F, deep, C, columns // C).transpose(0, 3, 1, 2, 4)
    bias_grads = jnp.concatenate(
        [
            all_bias_grad.reshape(3, T, F, -1)[0::2].transpose(1, 2, 0, 3).reshape(T, F, -1),
            up_bias_grad.reshape(T, F, -1),
            jnp.broadcast_to(out_bias_grad.reshape(1, F, deep), (T, F, deep)),
            jnp.broadcast_to(down_bias_grad.reshape(1, F, deep), (T, F, deep)),
        ],
        axis=2,
    ).astype(low)
    extra = bias_grads.shape[2] // deep
    bias_grads = jnp.pad(
        bias_grads.reshape(T, 1, F, deep, extra),
        ((0, 0), (0, C - 1), (0, 0), (0, 0), (0, 128 - extra)),
    )
    grads = jnp.concatenate([grads, bias_grads], axis=4)
    owned, latents_grad, mod_grads, cond_parts = reduce(
        mesh, grads, latents_grad.reshape(C, half, width), mod_grad, w_mod.transpose(1, 0, 2)
    )
    owned = owned.astype(full)
    wide = owned[:, :, : columns // C].transpose(1, 0, 2).reshape(deep, columns)
    own_bias = owned[0, :, columns // C : columns // C + extra].reshape(-1)
    qv_size, up_size = b_qv.size, up_projection_bias.size
    qkv_owned = wide[:, : 3 * part].reshape(deep, 3, part)
    out_owned = wide[:, 3 * part : 4 * part].T
    up_owned = wide[:, 4 * part : 4 * part + hidden]
    down_owned = wide[:, 4 * part + hidden :].T

    all_mod = mod_grads.transpose(2, 0, 1, 3, 4).reshape(F * group, 8, width)
    own_mod = lax.dynamic_slice_in_dim(all_mod, t * 3, 3, axis=1)
    cond_own = lax.dynamic_slice_in_dim(cond_all[:, :group], f * deep, deep, axis=2)
    mod_weight_grad = jnp.einsum(
        "ld,lkc->dkc", cond_own.reshape(F * group, deep), own_mod,
        precision=lax.Precision.HIGHEST,
    )
    mod_bias_grad = lax.dynamic_slice_in_dim(jnp.sum(own_mod, axis=0), f * deep, deep, axis=1)
    silu_total = cond_parts[:, :group, :deep].transpose(1, 0, 2).reshape(group, width)
    condition_grad = jax.vjp(jax.nn.silu, condition)[1](silu_total)[0]
    return (
        block_out,
        latents_grad,
        condition_grad,
        mod_weight_grad,
        mod_bias_grad,
        qkv_owned,
        own_bias[:qv_size].reshape(2, -1),
        out_owned,
        own_bias[qv_size + up_size : qv_size + up_size + deep],
        up_owned,
        own_bias[qv_size : qv_size + up_size],
        down_owned,
        own_bias[qv_size + up_size + deep : qv_size + up_size + 2 * deep],
    )


def solution(mesh):
    placed = (
        P("fsdp", "ctx", None),
        P("fsdp", None),
        P("fsdp", "tp", None),
        P("tp", "fsdp"),
        P("fsdp", None, "tp"),
        P(None, ("tp", "fsdp")),
        P("tp", "fsdp"),
        P("fsdp"),
        P("fsdp", "tp"),
        P(("tp", "fsdp")),
        P("tp", "fsdp"),
        P("fsdp"),
        P("fsdp", "ctx", None),
    )
    return jax.shard_map(
        functools.partial(shards, mesh),
        mesh=mesh,
        in_specs=placed,
        out_specs=(
            P("fsdp", "ctx", None),
            P("fsdp", "ctx", None),
            P("fsdp", None),
            P("fsdp", "tp", None),
            P("tp", "fsdp"),
            P("fsdp", None, "tp"),
            P(None, ("tp", "fsdp")),
            P("tp", "fsdp"),
            P("fsdp"),
            P("fsdp", "tp"),
            P(("tp", "fsdp")),
            P("tp", "fsdp"),
            P("fsdp"),
        ),
        check_vma=False,
    )
```

```python
import functools
import math

import jax
import jax.numpy as jnp
from jax import lax
from jax.experimental import pallas as pl
from jax.experimental.pallas import tpu as pltpu
from jax.sharding import PartitionSpec as P

HD = 64
EPSILON = 1e-06
MESH = pl.DeviceIdType.MESH


def normalize(values):
    centre = values - jnp.mean(values, axis=-1, keepdims=True)
    inverse = lax.rsqrt(jnp.mean(centre * centre, axis=-1, keepdims=True) + EPSILON)
    return (centre * inverse, inverse)


def norm_back(upstream, normed, inverse):
    return inverse * (
        upstream
        - jnp.mean(upstream, axis=-1, keepdims=True)
        - normed * jnp.mean(upstream * normed, axis=-1, keepdims=True)
    )


def remote(src, dst, send, recv, device):
    return pltpu.make_async_remote_copy(
        src_ref=src, dst_ref=dst, send_sem=send, recv_sem=recv,
        device_id=device, device_id_type=MESH,
    )


def greet(F, f, c, t):
    barrier = pltpu.get_barrier_semaphore()
    pl.semaphore_signal(barrier, inc=1, device_id={"tp": 1 - t}, device_id_type=MESH)
    pl.semaphore_signal(barrier, inc=1, device_id={"ctx": 1 - c}, device_id_type=MESH)

    def one(k, carry):
        pl.semaphore_signal(
            barrier, inc=1, device_id={"fsdp": lax.rem(f + k, F)}, device_id_type=MESH
        )
        return carry

    lax.fori_loop(1, F, one, 0)
    pl.semaphore_wait(barrier, F + 1)


def each_peer(F, f, body):
    def one(k, carry):
        body(k, lax.rem(f + k, F), lax.rem(f + F - k, F))
        return carry

    lax.fori_loop(1, F, one, 0)


def gather_kernel(
    F, C, T,
    w_ref, x_ref, ct_ref, sc_ref, bs_ref, wm_ref,
    W, X, CT, SC, BS, MO,
    MP, MR,
    w_s, w_r, wt_s, wt_r, sc_s, sc_r, bs_s, bs_r, m_s, m_r, big_s, big_r, loc,
):
    f, c, t = lax.axis_index("fsdp"), lax.axis_index("ctx"), lax.axis_index("tp")
    greet(F, f, c, t)
    other_core, other_half = {"tp": 1 - t}, {"ctx": 1 - c}

    def sc_copy(k, to, at):
        return remote(sc_ref, SC.at[at], sc_s.at[k], sc_r.at[at], {"fsdp": to})

    def bs_copy(k, to, at):
        return remote(bs_ref, BS.at[t, at], bs_s.at[k], bs_r.at[at], {"fsdp": to})

    part = w_ref.shape[2]
    columns = pl.ds(pl.multiple_of(t * part, 128), part)

    def place(at):
        return W.at[:, at, :, columns]

    def w_copy(k, to, at):
        return remote(w_ref, place(at), w_s.at[k], w_r.at[at], {"fsdp": to})

    def m_copy(k, to, at):
        return remote(MP.at[to], MR.at[at], m_s.at[k], m_r.at[at], {"fsdp": to})

    def core_copy(at):
        return remote(place(at), place(at), wt_s.at[at], wt_r.at[at], other_core)

    own_first = remote(w_ref, place(f), wt_s.at[f], wt_r.at[f], other_core)
    send_x = remote(x_ref.at[T * (1 - c) + t], X.at[c], big_s.at[0], big_r.at[0], other_half)
    send_ct = remote(ct_ref.at[T * (1 - c) + t], CT.at[c], big_s.at[1], big_r.at[1], other_half)
    keep_x = pltpu.make_async_copy(x_ref.at[T * c + t], X.at[c], loc.at[0])
    keep_ct = pltpu.make_async_copy(ct_ref.at[T * c + t], CT.at[c], loc.at[1])
    keep_w = pltpu.make_async_copy(w_ref, place(f), loc.at[2])

    def start_small(k, to, source):
        sc_copy(k, to, f).start()
        bs_copy(k, to, f).start()

    each_peer(F, f, start_small)
    each_peer(F, f, lambda k, to, source: w_copy(k, to, f).start())
    send_x.start()
    send_ct.start()
    own_first.start()
    keep_x.start()
    keep_ct.start()
    keep_w.start()
    SC[f] = sc_ref[...]
    BS[t, f] = bs_ref[...]
    each_peer(F, f, lambda k, to, source: sc_copy(k, to, source).wait_recv())
    rows = SC[...].reshape(F * SC.shape[1], SC.shape[2]).astype(jnp.bfloat16)
    MP[...] = jnp.dot(rows, wm_ref[...], preferred_element_type=jnp.float32).reshape(MP.shape)
    each_peer(F, f, lambda k, to, source: m_copy(k, to, f).start())
    MR[f] = MP[f]
    each_peer(F, f, lambda k, to, source: bs_copy(k, to, source).wait_recv())
    send_bs = remote(BS.at[t], BS.at[t], big_s.at[2], big_r.at[2], other_core)
    send_bs.start()
    each_peer(F, f, lambda k, to, source: m_copy(k, to, source).wait_recv())
    MO[t] = jnp.sum(MR[...], axis=0)
    send_mo = remote(MO.at[t], MO.at[t], big_s.at[3], big_r.at[3], other_core)
    send_mo.start()

    def forward(k, to, source):
        w_copy(k, to, source).wait_recv()
        core_copy(source).start()

    each_peer(F, f, forward)

    def finish(k, to, source):
        sc_copy(k, to, f).wait_send()
        bs_copy(k, to, f).wait_send()
        w_copy(k, to, f).wait_send()
        m_copy(k, to, f).wait_send()
        core_copy(source).wait()

    each_peer(F, f, finish)
    own_first.wait()
    send_x.wait()
    send_ct.wait()
    send_bs.wait()
    send_mo.wait()
    keep_x.wait()
    keep_ct.wait()
    keep_w.wait()


def gather(mesh, packed, latents, cotangent, cond_rows, biases, mod_weight):
    F, C, T = mesh.shape["fsdp"], mesh.shape["ctx"], mesh.shape["tp"]
    half, width = latents.shape[1:]
    rows, columns = cond_rows.shape[0], mod_weight.shape[1]
    anywhere = pl.BlockSpec(memory_space=pl.ANY)
    vmem = pl.BlockSpec(memory_space=pltpu.VMEM)
    dma = pltpu.SemaphoreType.DMA
    return pl.pallas_call(
        functools.partial(gather_kernel, F, C, T),
        out_shape=(
            jax.ShapeDtypeStruct((3, F, packed.shape[1], T * packed.shape[2]), packed.dtype),
            jax.ShapeDtypeStruct((C, half, width), jnp.float32),
            jax.ShapeDtypeStruct((C, half, width), jnp.float32),
            jax.ShapeDtypeStruct((F, rows, width), jnp.float32),
            jax.ShapeDtypeStruct((T, F) + biases.shape, jnp.float32),
            jax.ShapeDtypeStruct((T, rows, columns), jnp.float32),
        ),
        in_specs=[anywhere, anywhere, anywhere, vmem, vmem, vmem],
        out_specs=(anywhere, anywhere, anywhere, vmem, vmem, vmem),
        scratch_shapes=[
            pltpu.VMEM((F, rows, columns), jnp.float32),
            pltpu.VMEM((F, rows, columns), jnp.float32),
        ] + [dma((F,))] * 10 + [dma((4,)), dma((4,)), dma((3,))],
        compiler_params=pltpu.CompilerParams(
            collective_id=0, has_side_effects=True, vmem_limit_bytes=40 << 20
        ),
        name="gather",
    )(packed, latents, cotangent, cond_rows, biases, mod_weight)


def reduce_kernel(
    F, C, T,
    gp, gb, lg, here, landed, mg_ref, wm_ref,
    GO, BG, LO, BO, MG, CO,
    A, S1, B, S2, R, CP, CR, CX, GA, GS, GB, GT, GR,
    a_s, a_r, b_s, b_r, r_s, r_r, mg_s, mg_r, c_s, c_r, g_s, g_r, big_s, big_r, loc,
):
    f, c, t = lax.axis_index("fsdp"), lax.axis_index("ctx"), lax.axis_index("tp")
    deep = wm_ref.shape[1]
    greet(F, f, c, t)
    other_core, other_half = {"tp": 1 - t}, {"ctx": 1 - c}

    def mg_copy(k, to, at):
        return remote(mg_ref, MG.at[c, t, at], mg_s.at[k], mg_r.at[at], {"fsdp": to})

    wide = A.shape[4]

    def columns(core, h):
        return pl.ds(pl.multiple_of((core * C + h) * wide, 128), wide)

    def g_copy(to, at):
        return remote(GT.at[to], GR.at[at], g_s.at[to], g_r.at[at], {"fsdp": to})

    def a_copy(h, at):
        return remote(gp.at[:, at, :, columns(1 - t, h)], A.at[h, at], a_s.at[h, at], a_r.at[h, at], other_core)

    def b_copy(at):
        return remote(S1.at[1 - c, at], B.at[at], b_s.at[at], b_r.at[at], other_half)

    def r_copy(to, at):
        return remote(S2.at[to], R.at[at], r_s.at[to], r_r.at[at], {"fsdp": to})

    def c_copy(to, at):
        return remote(CP.at[to], CR.at[at], c_s.at[to], c_r.at[at], {"fsdp": to})

    def over_blocks(body):
        def one(k, carry):
            body(lax.rem(f + k, F))
            return carry

        lax.fori_loop(1, F + 1, one, 0)

    each_peer(F, f, lambda k, to, source: mg_copy(k, to, f).start())

    def start_a(at):
        a_copy(1 - c, at).start()
        a_copy(c, at).start()

    over_blocks(start_a)
    own = T * c + t
    paired = T * (1 - c) + t
    gb_core = remote(gb.at[1 - t], GA, big_s.at[7], big_r.at[7], other_core)
    gb_core.start()
    keep = pltpu.make_async_copy(lg.at[c], LO.at[own], loc.at[0])
    keep_here = pltpu.make_async_copy(here, BO.at[own], loc.at[1])
    keep_landed = pltpu.make_async_copy(landed, BO.at[paired], loc.at[2])
    keep.start()
    keep_here.start()
    keep_landed.start()
    MG[c, t, f] = mg_ref[...]

    def add(one, two):
        return (one.astype(jnp.float32) + two.astype(jnp.float32)).astype(jnp.bfloat16)

    def first(at):
        for away, h in enumerate((c, 1 - c)[::-1]):
            a_copy(h, at).wait_recv()
            S1[h, at] = add(gp[:, at, :, columns(t, h)], A[h, at])
            if away == 0:
                b_copy(at).start()

    over_blocks(first)
    send_lg = remote(lg.at[1 - c], LO.at[own], big_s.at[0], big_r.at[0], other_half)
    send_lg.start()
    gb_core.wait()
    GS[...] = gb[t] + GA[...]
    gb_half = remote(GS, GB, big_s.at[8], big_r.at[8], other_half)
    gb_half.start()
    share_here = remote(here, BO.at[own], big_s.at[9], big_r.at[9], other_core)
    share_landed = remote(landed, BO.at[paired], big_s.at[10], big_r.at[10], other_core)
    share_here.start()
    share_landed.start()
    each_peer(F, f, lambda k, to, source: mg_copy(k, to, source).wait_recv())
    mg_core = remote(MG.at[c, t], MG.at[c, t], big_s.at[1], big_r.at[1], other_core)
    mg_core.start()

    def second(at):
        b_copy(at).wait_recv()
        S2[at] = add(S1[c, at], B[at])

    def second_peer(k, to, source):
        second(to)
        r_copy(to, f).start()

    mg_core.wait()
    mg_half = remote(MG.at[c], MG.at[c], big_s.at[2], big_r.at[2], other_half)
    mg_half.start()
    each_peer(F, f, second_peer)
    second(f)
    mg_half.wait()
    gb_half.wait()
    GT[...] = GS[...] + GB[...]
    each_peer(F, f, lambda k, to, source: g_copy(to, f).start())
    GR[f] = GT[f]
    CP[...] = jnp.zeros_like(CP)
    for c2 in range(C):
        for t2 in range(T):
            total = jnp.zeros((F, deep), jnp.float32)
            for k in range(3):
                row = jnp.where(t == 0, MG[c2, t2, :, k, :], MG[c2, t2, :, 3 + k, :])
                total += lax.dot_general(
                    row, wm_ref[k].astype(jnp.float32), (((1,), (1,)), ((), ())),
                    precision=lax.Precision.HIGHEST, preferred_element_type=jnp.float32,
                )
            CP[:, T * c2 + t2, 0:deep] = total
    each_peer(F, f, lambda k, to, source: c_copy(to, f).start())
    CR[f] = CP[f]
    send_lg.wait_recv()
    keep.wait()

    def core_lg(n, at):
        return remote(LO.at[at], LO.at[at], big_s.at[3 + n], big_r.at[3 + n], other_core)

    core_lg(0, own).start()
    core_lg(1, T * (1 - c) + t).start()
    R[f] = S2[f]
    each_peer(F, f, lambda k, to, source: r_copy(to, source).wait_recv())
    total = lax.fori_loop(
        0, F, lambda k, sum_: sum_ + R[k].astype(jnp.float32),
        jnp.zeros(R.shape[1:], jnp.float32),
    )
    GO[c] = total.astype(jnp.bfloat16)
    go_half = remote(GO.at[c], GO.at[c], big_s.at[5], big_r.at[5], other_half)
    go_half.start()
    each_peer(F, f, lambda k, to, source: c_copy(to, source).wait_recv())
    c_core = remote(CR, CX, big_s.at[6], big_r.at[6], other_core)
    c_core.start()
    each_peer(F, f, lambda k, to, source: g_copy(to, source).wait_recv())
    BG[...] = jnp.sum(GR[...], axis=0)
    c_core.wait()
    CO[...] = CR[...] + CX[...]

    def finish(k, to, source):
        mg_copy(k, to, f).wait_send()
        r_copy(to, f).wait_send()
        c_copy(to, f).wait_send()
        g_copy(to, f).wait_send()

    each_peer(F, f, finish)

    def finish_block(at):
        a_copy(1 - c, at).wait_send()
        a_copy(c, at).wait_send()
        b_copy(at).wait_send()

    over_blocks(finish_block)
    send_lg.wait_send()
    go_half.wait()
    share_here.wait()
    share_landed.wait()
    keep_here.wait()
    keep_landed.wait()
    core_lg(0, own).wait()
    core_lg(1, T * (1 - c) + t).wait()


def reduce(mesh, grads, bias_grads, latents_grad, here, landed, mod_grad, mod_weight):
    F, C, T = mesh.shape["fsdp"], mesh.shape["ctx"], mesh.shape["tp"]
    half, width = latents_grad.shape[1:]
    block = (3, grads.shape[2], grads.shape[3] // (C * T))
    small = bias_grads.shape[2:]
    anywhere = pl.BlockSpec(memory_space=pl.ANY)
    vmem = pl.BlockSpec(memory_space=pltpu.VMEM)
    dma = pltpu.SemaphoreType.DMA
    low = jnp.bfloat16
    return pl.pallas_call(
        functools.partial(reduce_kernel, F, C, T),
        out_shape=(
            jax.ShapeDtypeStruct((C,) + block, low),
            jax.ShapeDtypeStruct(small, jnp.float32),
            jax.ShapeDtypeStruct((C * T, half, width), jnp.float32),
            jax.ShapeDtypeStruct((C * T, half, width), jnp.float32),
            jax.ShapeDtypeStruct((C, T, F) + mod_grad.shape, jnp.float32),
            jax.ShapeDtypeStruct((F, 8, 128), jnp.float32),
        ),
        in_specs=[vmem, vmem, anywhere, anywhere, anywhere, vmem, vmem],
        out_specs=(vmem, vmem, anywhere, anywhere, vmem, vmem),
        scratch_shapes=[
            pltpu.VMEM((C, F) + block, low),
            pltpu.VMEM((C, F) + block, low),
            pltpu.VMEM((F,) + block, low),
            pltpu.VMEM((F,) + block, low),
            pltpu.VMEM((F,) + block, low),
            pltpu.VMEM((F, 8, 128), jnp.float32),
            pltpu.VMEM((F, 8, 128), jnp.float32),
            pltpu.VMEM((F, 8, 128), jnp.float32),
            pltpu.VMEM((F,) + small, jnp.float32),
            pltpu.VMEM((F,) + small, jnp.float32),
            pltpu.VMEM((F,) + small, jnp.float32),
            pltpu.VMEM((F,) + small, jnp.float32),
            pltpu.VMEM((F,) + small, jnp.float32),
            dma((C, F)), dma((C, F)),
        ] + [dma((F,))] * 10 + [dma((11,)), dma((11,)), dma((3,))],
        compiler_params=pltpu.CompilerParams(
            collective_id=1, has_side_effects=True, vmem_limit_bytes=56 << 20
        ),
        name="reduce",
    )(grads, bias_grads, latents_grad, here, landed, mod_grad, mod_weight)


SCALE = 1.0 / math.sqrt(HD)
LOW = jnp.bfloat16


def head_columns(h, heads, part):
    base = (h // heads) * 4 * part + (h % heads) * HD
    return base, base + part, base + 2 * part


def forward_kernel(heads, part, rows_ref, all_ref, out_ref, log_ref):
    log_ref[...] = jnp.zeros_like(log_ref)
    for h in range(2 * heads):
        q, k, v = head_columns(h, heads, part)
        scores = dot_bt(all_ref[:, k : k + HD], rows_ref[:, q : q + HD]) * SCALE
        highest = jnp.max(scores, axis=0, keepdims=True)
        exponent = jnp.exp(scores - highest)
        totals = jnp.sum(exponent, axis=0, keepdims=True)
        softmax = (exponent * (1.0 / totals)).astype(LOW)
        mixed = dot_at(all_ref[:, v : v + HD], softmax)
        out_ref[:, h * HD : (h + 1) * HD] = mixed.T.astype(LOW)
        log_ref[h : h + 1, :] = highest + jnp.log(totals)


def backward_kernel(heads, part, rows_ref, all_ref, up_ref, log_ref, out_ref, k_sum, v_sum):
    step = pl.program_id(0)
    size = rows_ref.shape[0]
    here = pl.ds(pl.multiple_of(step * size, size), size)

    @pl.when(step == 0)
    def _():
        k_sum[...] = jnp.zeros_like(k_sum)
        v_sum[...] = jnp.zeros_like(v_sum)
        out_ref[...] = jnp.zeros_like(out_ref)

    for h in range(2 * heads):
        q, k, v = head_columns(h, heads, part)
        at = slice(h * HD, (h + 1) * HD)
        queries, upstream = rows_ref[:, q : q + HD], up_ref[:, at]
        keys = all_ref[:, k : k + HD]
        scores = dot_bt(keys, queries) * SCALE
        softmax = jnp.exp(scores - log_ref[h : h + 1, :])
        prob_grad = dot_bt(all_ref[:, v : v + HD], upstream)
        inner = jnp.sum(prob_grad * softmax, axis=0, keepdims=True)
        score_grad = (softmax * (prob_grad - inner)).astype(LOW)
        out_ref[here, q : q + HD] = (dot_at(keys, score_grad) * SCALE).T.astype(LOW)
        k_sum[:, at] += dot(score_grad, queries)
        v_sum[:, at] += dot(softmax.astype(LOW), upstream)

    @pl.when(step == pl.num_programs(0) - 1)
    def _():
        for h in range(2 * heads):
            q, k, v = head_columns(h, heads, part)
            at = slice(h * HD, (h + 1) * HD)
            out_ref[:, k : k + HD] = (k_sum[:, at] * SCALE).astype(LOW)
            out_ref[:, v : v + HD] = v_sum[:, at].astype(LOW)


def attention(projected, part):
    tokens, columns = projected.shape
    heads, size = part // HD, 256
    return pl.pallas_call(
        functools.partial(forward_kernel, heads, part),
        grid=(tokens // size,),
        out_shape=(
            jax.ShapeDtypeStruct((tokens, 2 * part), LOW),
            jax.ShapeDtypeStruct((8, tokens), jnp.float32),
        ),
        in_specs=[
            pl.BlockSpec((size, columns), lambda i: (i, 0)),
            pl.BlockSpec((tokens, columns), lambda i: (0, 0)),
        ],
        out_specs=(
            pl.BlockSpec((size, 2 * part), lambda i: (i, 0)),
            pl.BlockSpec((8, size), lambda i: (0, i)),
        ),
        compiler_params=pltpu.CompilerParams(vmem_limit_bytes=40 << 20),
        name="attention",
    )(projected, projected)


def attention_back(projected, upstream, log_totals, part):
    tokens, columns = projected.shape
    heads, size = part // HD, 256
    return pl.pallas_call(
        functools.partial(backward_kernel, heads, part),
        grid=(tokens // size,),
        out_shape=jax.ShapeDtypeStruct((tokens, columns), LOW),
        in_specs=[
            pl.BlockSpec((size, columns), lambda i: (i, 0)),
            pl.BlockSpec((tokens, columns), lambda i: (0, 0)),
            pl.BlockSpec((size, 2 * part), lambda i: (i, 0)),
            pl.BlockSpec((8, size), lambda i: (0, i)),
        ],
        out_specs=pl.BlockSpec((tokens, columns), lambda i: (0, 0)),
        scratch_shapes=[
            pltpu.VMEM((tokens, 2 * part), jnp.float32),
            pltpu.VMEM((tokens, 2 * part), jnp.float32),
        ],
        compiler_params=pltpu.CompilerParams(vmem_limit_bytes=40 << 20),
        name="attention_back",
    )(projected, projected, upstream, log_totals)


def dot(a, b):
    return jnp.dot(a, b, preferred_element_type=jnp.float32)


def dot_bt(a, b):
    return lax.dot_general(a, b, (((1,), (1,)), ((), ())), preferred_element_type=jnp.float32)


def dot_at(a, b):
    return lax.dot_general(a, b, (((0,), (0,)), ((), ())), preferred_element_type=jnp.float32)


def shards(
    mesh,
    latents_in,
    condition,
    w_mod,
    b_mod,
    w_qkv,
    b_qv,
    w_out,
    b_out,
    up_weight,
    up_projection_bias,
    down_weight,
    down_projection_bias,
    cotangent,
):
    F, C, T = mesh.shape["fsdp"], mesh.shape["ctx"], mesh.shape["tp"]
    f, c, t = lax.axis_index("fsdp"), lax.axis_index("ctx"), lax.axis_index("tp")
    group, half, width = latents_in.shape
    assert C == 2 and T == 2 and group == C * T
    deep = w_mod.shape[0]
    part = w_qkv.shape[2]
    hidden = up_weight.shape[1]
    low = jnp.bfloat16
    full = jnp.float32
    own = T * c + t

    assert hidden == 4 * part
    packed = jnp.stack(
        [
            jnp.concatenate([w_qkv.reshape(deep, 3 * part), w_out.T], axis=1),
            up_weight,
            down_weight.T,
        ]
    )
    flat_bias = jnp.concatenate(
        [
            b_mod.reshape(-1), b_qv.reshape(-1), b_out, up_projection_bias, down_projection_bias,
        ]
    ).astype(full)
    bias_rows = -(-flat_bias.shape[0] // 1024) * 8
    biases = jnp.pad(flat_bias, (0, bias_rows * 128 - flat_bias.shape[0])).reshape(bias_rows, 128)
    silu_cond = jax.nn.silu(condition).astype(low)
    cond_rows = jnp.pad(silu_cond.astype(full), ((0, 8 - group), (0, 0)))
    mod_padded = lax.dynamic_update_slice(
        jnp.zeros((width, 3 * width), low), w_mod.reshape(deep, 3 * width), (f * deep, 0)
    )
    weights, x, cot, cond_all, bias_all, mod_all = gather(
        mesh, packed, latents_in, cotangent, cond_rows, biases, mod_padded
    )
    x = x.reshape(C * half, width)
    cot = cot.reshape(C * half, width)
    weights = weights.reshape(3, width, T * hidden)
    qkvo_full, up_full, down_t = weights[0], weights[1], weights[2]
    outs_t = qkvo_full.reshape(width, T, 4 * part)[:, :, 3 * part :].reshape(width, width)

    bias_all = bias_all.reshape(T, F, -1)
    edges = [3 * deep, b_qv.size, b_out.size, up_projection_bias.size, down_projection_bias.size]
    pieces, start = [], 0
    for size in edges:
        pieces.append(bias_all[:, :, start : start + size])
        start += size
    mod_bias = pieces[0].reshape(T, F, 3, deep).transpose(0, 2, 1, 3).reshape(6, width)
    qv_bias = pieces[1].reshape(T, F, 2, -1).transpose(0, 2, 1, 3).reshape(T, 2, part)
    no_bias = jnp.zeros((T, part), full)
    qkvo_bias = jnp.concatenate([qv_bias[:, 0], no_bias, qv_bias[:, 1], no_bias], axis=1)
    out_bias = pieces[2][0].reshape(width)
    up_bias = pieces[3].reshape(T * hidden)
    down_bias = pieces[4][0].reshape(width)

    modulation = lax.dynamic_index_in_dim(mod_all, own, 1, keepdims=False)
    modulation = modulation.reshape(6, width) + mod_bias
    shift_one, scale_one, gate_one, shift_two, scale_two, gate_two = (
        modulation[k : k + 1] for k in range(6)
    )

    normed_one, inverse_one = normalize(x)
    hidden_one = (normed_one * (1.0 + scale_one) + shift_one).astype(low)
    projected = (dot(hidden_one, qkvo_full) + qkvo_bias.reshape(1, T * hidden)).astype(low)
    attended, log_totals = attention(projected, part)
    branch = dot_bt(attended, outs_t) + out_bias
    middle = x + gate_one * branch
    normed_two, inverse_two = normalize(middle)
    hidden_two = (normed_two * (1.0 + scale_two) + shift_two).astype(low)
    upper_in = dot(hidden_two, up_full) + up_bias
    gelu_value, gelu_pull = jax.vjp(lambda u: jax.nn.gelu(u, approximate=True), upper_in)
    active = gelu_value.astype(low)
    mlp_out = dot_bt(active, down_t) + down_bias
    block_own = (middle + gate_two * mlp_out).reshape(C, half, width)

    away = lax.dynamic_index_in_dim(block_own, 1 - c, 0, keepdims=False)
    here = lax.dynamic_index_in_dim(block_own, c, 0, keepdims=False)
    landed = lax.ppermute(away, "ctx", [(0, 1), (1, 0)])

    gate_two_grad = jnp.sum(cot * mlp_out, axis=0)
    down_in = (cot * gate_two).astype(low)
    down_bias_grad = jnp.sum(down_in, axis=0, dtype=full)
    down_grad_t = dot_at(down_in, active)
    upper_grad = gelu_pull(dot(down_in, down_t))[0].astype(low)
    up_bias_grad = jnp.sum(upper_grad, axis=0, dtype=full)
    up_grad = dot_at(hidden_two, upper_grad)
    hidden_two_grad = dot_bt(upper_grad, up_full)
    scale_two_grad = jnp.sum(hidden_two_grad * normed_two, axis=0)
    shift_two_grad = jnp.sum(hidden_two_grad, axis=0)
    middle_grad = cot + norm_back(hidden_two_grad * (1.0 + scale_two), normed_two, inverse_two)
    gate_one_grad = jnp.sum(middle_grad * branch, axis=0)
    branch_grad = (middle_grad * gate_one).astype(low)
    out_bias_grad = jnp.sum(branch_grad, axis=0, dtype=full)
    out_grad_t = dot_at(branch_grad, attended)
    attended_grad = dot(branch_grad, outs_t).astype(low)
    projected_grad = attention_back(projected, attended_grad, log_totals, part)
    all_bias_grad = jnp.sum(projected_grad, axis=0, dtype=full)
    qkvo_grad = dot_at(hidden_one, projected_grad).reshape(width, T, 4 * part)
    qkvo_grad = jnp.concatenate(
        [qkvo_grad[:, :, : 3 * part], out_grad_t.reshape(width, T, part)], axis=2
    ).reshape(width, T * hidden)
    hidden_one_grad = dot_bt(projected_grad, qkvo_full)
    scale_one_grad = jnp.sum(hidden_one_grad * normed_one, axis=0)
    shift_one_grad = jnp.sum(hidden_one_grad, axis=0)
    latents_grad = middle_grad + norm_back(
        hidden_one_grad * (1.0 + scale_one), normed_one, inverse_one
    )
    zeros = jnp.zeros((width,), full)
    mod_grad = jnp.stack(
        [
            shift_one_grad, scale_one_grad, gate_one_grad,
            shift_two_grad, scale_two_grad, gate_two_grad, zeros, zeros,
        ]
    )

    grads = jnp.stack([g.astype(low) for g in (qkvo_grad, up_grad, down_grad_t)])
    grads = grads.reshape(3, F, deep, T * hidden)
    bias_grads = jnp.concatenate(
        [
            all_bias_grad.reshape(T, 4, F, -1)[:, 0:3:2].transpose(0, 2, 1, 3).reshape(T, F, -1),
            up_bias_grad.reshape(T, F, -1),
            jnp.broadcast_to(out_bias_grad.reshape(1, F, deep), (T, F, deep)),
            jnp.broadcast_to(down_bias_grad.reshape(1, F, deep), (T, F, deep)),
        ],
        axis=2,
    )
    count = bias_grads.shape[2]
    bias_grads = jnp.pad(bias_grads, ((0, 0), (0, 0), (0, 1024 * -(-count // 1024) - count)))
    owned, own_bias, latents_grad, block_out, mod_grads, cond_parts = reduce(
        mesh, grads, bias_grads.reshape(T, F, -1, 128), latents_grad.reshape(C, half, width),
        here, landed, mod_grad, w_mod.transpose(1, 0, 2),
    )
    owned = owned.astype(full).transpose(1, 2, 0, 3).reshape(3, deep, hidden)
    own_bias = own_bias.reshape(-1)
    qv_size, up_size = b_qv.size, up_projection_bias.size
    qkv_owned = owned[0, :, : 3 * part].reshape(deep, 3, part)
    out_owned = owned[0, :, 3 * part :].T
    up_owned = owned[1]
    down_owned = owned[2].T

    all_mod = mod_grads.transpose(2, 0, 1, 3, 4).reshape(F * group, 8, width)
    own_mod = lax.dynamic_slice_in_dim(all_mod, t * 3, 3, axis=1)
    cond_own = lax.dynamic_slice_in_dim(cond_all[:, :group], f * deep, deep, axis=2)
    mod_weight_grad = jnp.einsum(
        "ld,lkc->dkc", cond_own.reshape(F * group, deep), own_mod,
        precision=lax.Precision.HIGHEST,
    )
    mod_bias_grad = lax.dynamic_slice_in_dim(jnp.sum(own_mod, axis=0), f * deep, deep, axis=1)
    silu_total = cond_parts[:, :group, :deep].transpose(1, 0, 2).reshape(group, width)
    condition_grad = jax.vjp(jax.nn.silu, condition)[1](silu_total)[0]
    return (
        block_out,
        latents_grad,
        condition_grad,
        mod_weight_grad,
        mod_bias_grad,
        qkv_owned,
        own_bias[:qv_size].reshape(2, -1),
        out_owned,
        own_bias[qv_size + up_size : qv_size + up_size + deep],
        up_owned,
        own_bias[qv_size : qv_size + up_size],
        down_owned,
        own_bias[qv_size + up_size + deep : qv_size + up_size + 2 * deep],
    )


def solution(mesh):
    placed = (
        P("fsdp", "ctx", None),
        P("fsdp", None),
        P("fsdp", "tp", None),
        P("tp", "fsdp"),
        P("fsdp", None, "tp"),
        P(None, ("tp", "fsdp")),
        P("tp", "fsdp"),
        P("fsdp"),
        P("fsdp", "tp"),
        P(("tp", "fsdp")),
        P("tp", "fsdp"),
        P("fsdp"),
        P("fsdp", "ctx", None),
    )
    return jax.shard_map(
        functools.partial(shards, mesh),
        mesh=mesh,
        in_specs=placed,
        out_specs=(
            P("fsdp", "ctx", None),
            P("fsdp", "ctx", None),
            P("fsdp", None),
            P("fsdp", "tp", None),
            P("tp", "fsdp"),
            P("fsdp", None, "tp"),
            P(None, ("tp", "fsdp")),
            P("tp", "fsdp"),
            P("fsdp"),
            P("fsdp", "tp"),
            P(("tp", "fsdp")),
            P("tp", "fsdp"),
            P("fsdp"),
        ),
        check_vma=False,
    )
```

```python
import functools
import math

import jax
import jax.numpy as jnp
from jax import lax
from jax.experimental import pallas as pl
from jax.experimental.pallas import tpu as pltpu
from jax.sharding import PartitionSpec as P

HD = 64
EPSILON = 1e-06
MESH = pl.DeviceIdType.MESH


def normalize(values):
    centre = values - jnp.mean(values, axis=-1, keepdims=True)
    inverse = lax.rsqrt(jnp.mean(centre * centre, axis=-1, keepdims=True) + EPSILON)
    return (centre * inverse, inverse)


def norm_back(upstream, normed, inverse):
    return inverse * (
        upstream
        - jnp.mean(upstream, axis=-1, keepdims=True)
        - normed * jnp.mean(upstream * normed, axis=-1, keepdims=True)
    )


def remote(src, dst, send, recv, device):
    return pltpu.make_async_remote_copy(
        src_ref=src, dst_ref=dst, send_sem=send, recv_sem=recv,
        device_id=device, device_id_type=MESH,
    )


def greet(F, f, c, t):
    barrier = pltpu.get_barrier_semaphore()
    pl.semaphore_signal(barrier, inc=1, device_id={"tp": 1 - t}, device_id_type=MESH)
    pl.semaphore_signal(barrier, inc=1, device_id={"ctx": 1 - c}, device_id_type=MESH)

    def one(k, carry):
        pl.semaphore_signal(
            barrier, inc=1, device_id={"fsdp": lax.rem(f + k, F)}, device_id_type=MESH
        )
        return carry

    lax.fori_loop(1, F, one, 0)
    pl.semaphore_wait(barrier, F + 1)


def each_peer(F, f, body):
    def one(k, carry):
        body(k, lax.rem(f + k, F), lax.rem(f + F - k, F))
        return carry

    lax.fori_loop(1, F, one, 0)


def gather_kernel(
    F, C, T,
    w_ref, x_ref, ct_ref, sc_ref, bs_ref, wm_ref,
    W, X, CT, SC, BS, MO,
    MP, MR,
    w_s, w_r, wt_s, wt_r, sc_s, sc_r, bs_s, bs_r, m_s, m_r, big_s, big_r, loc,
):
    f, c, t = lax.axis_index("fsdp"), lax.axis_index("ctx"), lax.axis_index("tp")
    greet(F, f, c, t)
    other_core, other_half = {"tp": 1 - t}, {"ctx": 1 - c}

    def sc_copy(k, to, at):
        return remote(sc_ref, SC.at[at], sc_s.at[k], sc_r.at[at], {"fsdp": to})

    def bs_copy(k, to, at):
        return remote(bs_ref, BS.at[t, at], bs_s.at[k], bs_r.at[at], {"fsdp": to})

    part = w_ref.shape[2]
    columns = pl.ds(pl.multiple_of(t * part, 128), part)

    def place(at):
        return W.at[:, at, :, columns]

    def w_copy(k, to, at):
        return remote(w_ref, place(at), w_s.at[k], w_r.at[at], {"fsdp": to})

    def m_copy(k, to, at):
        return remote(MP.at[to], MR.at[at], m_s.at[k], m_r.at[at], {"fsdp": to})

    def core_copy(at):
        return remote(place(at), place(at), wt_s.at[at], wt_r.at[at], other_core)

    own_first = remote(w_ref, place(f), wt_s.at[f], wt_r.at[f], other_core)
    send_x = remote(x_ref.at[T * (1 - c) + t], X.at[c], big_s.at[0], big_r.at[0], other_half)
    send_ct = remote(ct_ref.at[T * (1 - c) + t], CT.at[c], big_s.at[1], big_r.at[1], other_half)
    keep_x = pltpu.make_async_copy(x_ref.at[T * c + t], X.at[c], loc.at[0])
    keep_ct = pltpu.make_async_copy(ct_ref.at[T * c + t], CT.at[c], loc.at[1])
    keep_w = pltpu.make_async_copy(w_ref, place(f), loc.at[2])

    def start_small(k, to, source):
        sc_copy(k, to, f).start()
        bs_copy(k, to, f).start()

    each_peer(F, f, start_small)
    each_peer(F, f, lambda k, to, source: w_copy(k, to, f).start())
    send_x.start()
    send_ct.start()
    own_first.start()
    keep_x.start()
    keep_ct.start()
    keep_w.start()
    SC[f] = sc_ref[...]
    BS[t, f] = bs_ref[...]
    each_peer(F, f, lambda k, to, source: sc_copy(k, to, source).wait_recv())
    rows = SC[...].reshape(F * SC.shape[1], SC.shape[2]).astype(jnp.bfloat16)
    MP[...] = jnp.dot(rows, wm_ref[...], preferred_element_type=jnp.float32).reshape(MP.shape)
    each_peer(F, f, lambda k, to, source: m_copy(k, to, f).start())
    MR[f] = MP[f]
    each_peer(F, f, lambda k, to, source: bs_copy(k, to, source).wait_recv())
    send_bs = remote(BS.at[t], BS.at[t], big_s.at[2], big_r.at[2], other_core)
    send_bs.start()
    each_peer(F, f, lambda k, to, source: m_copy(k, to, source).wait_recv())
    MO[t] = jnp.sum(MR[...], axis=0)
    send_mo = remote(MO.at[t], MO.at[t], big_s.at[3], big_r.at[3], other_core)
    send_mo.start()

    def forward(k, to, source):
        w_copy(k, to, source).wait_recv()
        core_copy(source).start()

    each_peer(F, f, forward)

    def finish(k, to, source):
        sc_copy(k, to, f).wait_send()
        bs_copy(k, to, f).wait_send()
        w_copy(k, to, f).wait_send()
        m_copy(k, to, f).wait_send()
        core_copy(source).wait()

    each_peer(F, f, finish)
    own_first.wait()
    send_x.wait()
    send_ct.wait()
    send_bs.wait()
    send_mo.wait()
    keep_x.wait()
    keep_ct.wait()
    keep_w.wait()


def gather(mesh, packed, latents, cotangent, cond_rows, biases, mod_weight):
    F, C, T = mesh.shape["fsdp"], mesh.shape["ctx"], mesh.shape["tp"]
    half, width = latents.shape[1:]
    rows, columns = cond_rows.shape[0], mod_weight.shape[1]
    anywhere = pl.BlockSpec(memory_space=pl.ANY)
    vmem = pl.BlockSpec(memory_space=pltpu.VMEM)
    dma = pltpu.SemaphoreType.DMA
    return pl.pallas_call(
        functools.partial(gather_kernel, F, C, T),
        out_shape=(
            jax.ShapeDtypeStruct((3, F, packed.shape[1], T * packed.shape[2]), packed.dtype),
            jax.ShapeDtypeStruct((C, half, width), latents.dtype),
            jax.ShapeDtypeStruct((C, half, width), latents.dtype),
            jax.ShapeDtypeStruct((F, rows, width), jnp.float32),
            jax.ShapeDtypeStruct((T, F) + biases.shape, jnp.float32),
            jax.ShapeDtypeStruct((T, rows, columns), jnp.float32),
        ),
        in_specs=[anywhere, anywhere, anywhere, vmem, vmem, vmem],
        out_specs=(anywhere, anywhere, anywhere, vmem, vmem, vmem),
        scratch_shapes=[
            pltpu.VMEM((F, rows, columns), jnp.float32),
            pltpu.VMEM((F, rows, columns), jnp.float32),
        ] + [dma((F,))] * 10 + [dma((4,)), dma((4,)), dma((3,))],
        compiler_params=pltpu.CompilerParams(
            collective_id=0, has_side_effects=True, vmem_limit_bytes=40 << 20
        ),
        name="gather",
    )(packed, latents, cotangent, cond_rows, biases, mod_weight)


def reduce_kernel(
    F, C, T,
    gp, gb, lg, here, landed, mg_ref, wm_ref,
    GO, BG, LO, BO, MG, CO,
    A, S1, B, S2, R, CP, CR, CX, GA, GS, GB, GT, GR,
    a_s, a_r, b_s, b_r, r_s, r_r, mg_s, mg_r, c_s, c_r, g_s, g_r, big_s, big_r, loc,
):
    f, c, t = lax.axis_index("fsdp"), lax.axis_index("ctx"), lax.axis_index("tp")
    deep = wm_ref.shape[1]
    greet(F, f, c, t)
    other_core, other_half = {"tp": 1 - t}, {"ctx": 1 - c}

    def mg_copy(k, to, at):
        return remote(mg_ref, MG.at[c, t, at], mg_s.at[k], mg_r.at[at], {"fsdp": to})

    wide = A.shape[4]

    def columns(core, h):
        return pl.ds(pl.multiple_of((core * C + h) * wide, 128), wide)

    def g_copy(to, at):
        return remote(GT.at[to], GR.at[at], g_s.at[to], g_r.at[at], {"fsdp": to})

    def a_copy(h, at):
        return remote(gp.at[:, at, :, columns(1 - t, h)], A.at[h, at], a_s.at[h, at], a_r.at[h, at], other_core)

    def b_copy(at):
        return remote(S1.at[1 - c, at], B.at[at], b_s.at[at], b_r.at[at], other_half)

    def r_copy(to, at):
        return remote(S2.at[to], R.at[at], r_s.at[to], r_r.at[at], {"fsdp": to})

    def c_copy(to, at):
        return remote(CP.at[to], CR.at[at], c_s.at[to], c_r.at[at], {"fsdp": to})

    def over_blocks(body):
        def one(k, carry):
            body(lax.rem(f + k, F))
            return carry

        lax.fori_loop(1, F + 1, one, 0)

    each_peer(F, f, lambda k, to, source: mg_copy(k, to, f).start())

    def start_a(at):
        a_copy(1 - c, at).start()
        a_copy(c, at).start()

    over_blocks(start_a)
    own = T * c + t
    paired = T * (1 - c) + t
    gb_core = remote(gb.at[1 - t], GA, big_s.at[7], big_r.at[7], other_core)
    gb_core.start()
    keep = pltpu.make_async_copy(lg.at[c], LO.at[own], loc.at[0])
    keep_here = pltpu.make_async_copy(here, BO.at[own], loc.at[1])
    keep_landed = pltpu.make_async_copy(landed, BO.at[paired], loc.at[2])
    keep.start()
    keep_here.start()
    keep_landed.start()
    MG[c, t, f] = mg_ref[...]

    def add(one, two):
        return (one.astype(jnp.float32) + two.astype(jnp.float32)).astype(jnp.bfloat16)

    def first(at):
        for away, h in enumerate((c, 1 - c)[::-1]):
            a_copy(h, at).wait_recv()
            S1[h, at] = add(gp[:, at, :, columns(t, h)], A[h, at])
            if away == 0:
                b_copy(at).start()

    over_blocks(first)
    send_lg = remote(lg.at[1 - c], LO.at[own], big_s.at[0], big_r.at[0], other_half)
    send_lg.start()
    gb_core.wait()
    GS[...] = gb[t] + GA[...]
    gb_half = remote(GS, GB, big_s.at[8], big_r.at[8], other_half)
    gb_half.start()
    share_here = remote(here, BO.at[own], big_s.at[9], big_r.at[9], other_core)
    share_landed = remote(landed, BO.at[paired], big_s.at[10], big_r.at[10], other_core)
    share_here.start()
    share_landed.start()
    each_peer(F, f, lambda k, to, source: mg_copy(k, to, source).wait_recv())
    mg_core = remote(MG.at[c, t], MG.at[c, t], big_s.at[1], big_r.at[1], other_core)
    mg_core.start()

    def second(at):
        b_copy(at).wait_recv()
        S2[at] = add(S1[c, at], B[at])

    def second_peer(k, to, source):
        second(to)
        r_copy(to, f).start()

    mg_core.wait()
    mg_half = remote(MG.at[c], MG.at[c], big_s.at[2], big_r.at[2], other_half)
    mg_half.start()
    each_peer(F, f, second_peer)
    second(f)
    mg_half.wait()
    gb_half.wait()
    GT[...] = GS[...] + GB[...]
    each_peer(F, f, lambda k, to, source: g_copy(to, f).start())
    GR[f] = GT[f]
    CP[...] = jnp.zeros_like(CP)
    for c2 in range(C):
        for t2 in range(T):
            total = jnp.zeros((F, deep), jnp.float32)
            for k in range(3):
                row = jnp.where(t == 0, MG[c2, t2, :, k, :], MG[c2, t2, :, 3 + k, :])
                total += lax.dot_general(
                    row, wm_ref[k].astype(jnp.float32), (((1,), (1,)), ((), ())),
                    precision=lax.Precision.HIGHEST, preferred_element_type=jnp.float32,
                )
            CP[:, T * c2 + t2, 0:deep] = total
    each_peer(F, f, lambda k, to, source: c_copy(to, f).start())
    CR[f] = CP[f]
    send_lg.wait_recv()
    keep.wait()

    def core_lg(n, at):
        return remote(LO.at[at], LO.at[at], big_s.at[3 + n], big_r.at[3 + n], other_core)

    core_lg(0, own).start()
    core_lg(1, T * (1 - c) + t).start()
    R[f] = S2[f]
    each_peer(F, f, lambda k, to, source: r_copy(to, source).wait_recv())
    total = lax.fori_loop(
        0, F, lambda k, sum_: sum_ + R[k].astype(jnp.float32),
        jnp.zeros(R.shape[1:], jnp.float32),
    )
    GO[c] = total.astype(jnp.bfloat16)
    go_half = remote(GO.at[c], GO.at[c], big_s.at[5], big_r.at[5], other_half)
    go_half.start()
    each_peer(F, f, lambda k, to, source: c_copy(to, source).wait_recv())
    c_core = remote(CR, CX, big_s.at[6], big_r.at[6], other_core)
    c_core.start()
    each_peer(F, f, lambda k, to, source: g_copy(to, source).wait_recv())
    BG[...] = jnp.sum(GR[...], axis=0)
    c_core.wait()
    CO[...] = CR[...] + CX[...]

    def finish(k, to, source):
        mg_copy(k, to, f).wait_send()
        r_copy(to, f).wait_send()
        c_copy(to, f).wait_send()
        g_copy(to, f).wait_send()

    each_peer(F, f, finish)

    def finish_block(at):
        a_copy(1 - c, at).wait_send()
        a_copy(c, at).wait_send()
        b_copy(at).wait_send()

    over_blocks(finish_block)
    send_lg.wait_send()
    go_half.wait()
    share_here.wait()
    share_landed.wait()
    keep_here.wait()
    keep_landed.wait()
    core_lg(0, own).wait()
    core_lg(1, T * (1 - c) + t).wait()


def reduce(mesh, grads, bias_grads, latents_grad, here, landed, mod_grad, mod_weight):
    F, C, T = mesh.shape["fsdp"], mesh.shape["ctx"], mesh.shape["tp"]
    half, width = latents_grad.shape[1:]
    block = (3, grads.shape[2], grads.shape[3] // (C * T))
    small = bias_grads.shape[2:]
    anywhere = pl.BlockSpec(memory_space=pl.ANY)
    vmem = pl.BlockSpec(memory_space=pltpu.VMEM)
    dma = pltpu.SemaphoreType.DMA
    low = jnp.bfloat16
    return pl.pallas_call(
        functools.partial(reduce_kernel, F, C, T),
        out_shape=(
            jax.ShapeDtypeStruct((C,) + block, low),
            jax.ShapeDtypeStruct(small, jnp.float32),
            jax.ShapeDtypeStruct((C * T, half, width), low),
            jax.ShapeDtypeStruct((C * T, half, width), low),
            jax.ShapeDtypeStruct((C, T, F) + mod_grad.shape, jnp.float32),
            jax.ShapeDtypeStruct((F, 8, 128), jnp.float32),
        ),
        in_specs=[vmem, vmem, anywhere, anywhere, anywhere, vmem, vmem],
        out_specs=(vmem, vmem, anywhere, anywhere, vmem, vmem),
        scratch_shapes=[
            pltpu.VMEM((C, F) + block, low),
            pltpu.VMEM((C, F) + block, low),
            pltpu.VMEM((F,) + block, low),
            pltpu.VMEM((F,) + block, low),
            pltpu.VMEM((F,) + block, low),
            pltpu.VMEM((F, 8, 128), jnp.float32),
            pltpu.VMEM((F, 8, 128), jnp.float32),
            pltpu.VMEM((F, 8, 128), jnp.float32),
            pltpu.VMEM((F,) + small, jnp.float32),
            pltpu.VMEM((F,) + small, jnp.float32),
            pltpu.VMEM((F,) + small, jnp.float32),
            pltpu.VMEM((F,) + small, jnp.float32),
            pltpu.VMEM((F,) + small, jnp.float32),
            dma((C, F)), dma((C, F)),
        ] + [dma((F,))] * 10 + [dma((11,)), dma((11,)), dma((3,))],
        compiler_params=pltpu.CompilerParams(
            collective_id=1, has_side_effects=True, vmem_limit_bytes=56 << 20
        ),
        name="reduce",
    )(grads, bias_grads, latents_grad, here, landed, mod_grad, mod_weight)


SCALE = 1.0 / math.sqrt(HD)
LOW = jnp.bfloat16


def head_columns(h, heads, part):
    base = (h // heads) * 4 * part + (h % heads) * HD
    return base, base + part, base + 2 * part


def forward_kernel(heads, part, rows_ref, all_ref, out_ref, log_ref):
    log_ref[...] = jnp.zeros_like(log_ref)
    for h in range(2 * heads):
        q, k, v = head_columns(h, heads, part)
        scores = dot_bt(all_ref[:, k : k + HD], rows_ref[:, q : q + HD]) * SCALE
        highest = jnp.max(scores, axis=0, keepdims=True)
        exponent = jnp.exp(scores - highest)
        totals = jnp.sum(exponent, axis=0, keepdims=True)
        softmax = (exponent * (1.0 / totals)).astype(LOW)
        mixed = dot_at(all_ref[:, v : v + HD], softmax)
        out_ref[:, h * HD : (h + 1) * HD] = mixed.T.astype(LOW)
        log_ref[h : h + 1, :] = highest + jnp.log(totals)


def backward_kernel(heads, part, rows_ref, all_ref, up_ref, log_ref, out_ref, k_sum, v_sum):
    step = pl.program_id(0)
    size = rows_ref.shape[0]
    here = pl.ds(pl.multiple_of(step * size, size), size)

    @pl.when(step == 0)
    def _():
        k_sum[...] = jnp.zeros_like(k_sum)
        v_sum[...] = jnp.zeros_like(v_sum)
        out_ref[...] = jnp.zeros_like(out_ref)

    for h in range(2 * heads):
        q, k, v = head_columns(h, heads, part)
        at = slice(h * HD, (h + 1) * HD)
        queries, upstream = rows_ref[:, q : q + HD], up_ref[:, at]
        keys = all_ref[:, k : k + HD]
        scores = dot_bt(keys, queries) * SCALE
        softmax = jnp.exp(scores - log_ref[h : h + 1, :])
        prob_grad = dot_bt(all_ref[:, v : v + HD], upstream)
        inner = jnp.sum(prob_grad * softmax, axis=0, keepdims=True)
        score_grad = (softmax * (prob_grad - inner)).astype(LOW)
        out_ref[here, q : q + HD] = (dot_at(keys, score_grad) * SCALE).T.astype(LOW)
        k_sum[:, at] += dot(score_grad, queries)
        v_sum[:, at] += dot(softmax.astype(LOW), upstream)

    @pl.when(step == pl.num_programs(0) - 1)
    def _():
        for h in range(2 * heads):
            q, k, v = head_columns(h, heads, part)
            at = slice(h * HD, (h + 1) * HD)
            out_ref[:, k : k + HD] = (k_sum[:, at] * SCALE).astype(LOW)
            out_ref[:, v : v + HD] = v_sum[:, at].astype(LOW)


def attention(projected, part):
    tokens, columns = projected.shape
    heads, size = part // HD, 256
    return pl.pallas_call(
        functools.partial(forward_kernel, heads, part),
        grid=(tokens // size,),
        out_shape=(
            jax.ShapeDtypeStruct((tokens, 2 * part), LOW),
            jax.ShapeDtypeStruct((8, tokens), jnp.float32),
        ),
        in_specs=[
            pl.BlockSpec((size, columns), lambda i: (i, 0)),
            pl.BlockSpec((tokens, columns), lambda i: (0, 0)),
        ],
        out_specs=(
            pl.BlockSpec((size, 2 * part), lambda i: (i, 0)),
            pl.BlockSpec((8, size), lambda i: (0, i)),
        ),
        compiler_params=pltpu.CompilerParams(vmem_limit_bytes=40 << 20),
        name="attention",
    )(projected, projected)


def attention_back(projected, upstream, log_totals, part):
    tokens, columns = projected.shape
    heads, size = part // HD, 256
    return pl.pallas_call(
        functools.partial(backward_kernel, heads, part),
        grid=(tokens // size,),
        out_shape=jax.ShapeDtypeStruct((tokens, columns), LOW),
        in_specs=[
            pl.BlockSpec((size, columns), lambda i: (i, 0)),
            pl.BlockSpec((tokens, columns), lambda i: (0, 0)),
            pl.BlockSpec((size, 2 * part), lambda i: (i, 0)),
            pl.BlockSpec((8, size), lambda i: (0, i)),
        ],
        out_specs=pl.BlockSpec((tokens, columns), lambda i: (0, 0)),
        scratch_shapes=[
            pltpu.VMEM((tokens, 2 * part), jnp.float32),
            pltpu.VMEM((tokens, 2 * part), jnp.float32),
        ],
        compiler_params=pltpu.CompilerParams(vmem_limit_bytes=40 << 20),
        name="attention_back",
    )(projected, projected, upstream, log_totals)


def dot(a, b):
    return jnp.dot(a, b, preferred_element_type=jnp.float32)


def dot_bt(a, b):
    return lax.dot_general(a, b, (((1,), (1,)), ((), ())), preferred_element_type=jnp.float32)


def dot_at(a, b):
    return lax.dot_general(a, b, (((0,), (0,)), ((), ())), preferred_element_type=jnp.float32)


def shards(
    mesh,
    latents_in,
    condition,
    w_mod,
    b_mod,
    w_qkv,
    b_qv,
    w_out,
    b_out,
    up_weight,
    up_projection_bias,
    down_weight,
    down_projection_bias,
    cotangent,
):
    F, C, T = mesh.shape["fsdp"], mesh.shape["ctx"], mesh.shape["tp"]
    f, c, t = lax.axis_index("fsdp"), lax.axis_index("ctx"), lax.axis_index("tp")
    group, half, width = latents_in.shape
    assert C == 2 and T == 2 and group == C * T
    deep = w_mod.shape[0]
    part = w_qkv.shape[2]
    hidden = up_weight.shape[1]
    low = jnp.bfloat16
    full = jnp.float32
    own = T * c + t

    assert hidden == 4 * part
    packed = jnp.stack(
        [
            jnp.concatenate([w_qkv.reshape(deep, 3 * part), w_out.T], axis=1),
            up_weight,
            down_weight.T,
        ]
    )
    flat_bias = jnp.concatenate(
        [
            b_mod.reshape(-1), b_qv.reshape(-1), b_out, up_projection_bias, down_projection_bias,
        ]
    ).astype(full)
    bias_rows = -(-flat_bias.shape[0] // 1024) * 8
    biases = jnp.pad(flat_bias, (0, bias_rows * 128 - flat_bias.shape[0])).reshape(bias_rows, 128)
    silu_cond = jax.nn.silu(condition).astype(low)
    cond_rows = jnp.pad(silu_cond.astype(full), ((0, 8 - group), (0, 0)))
    mod_padded = lax.dynamic_update_slice(
        jnp.zeros((width, 3 * width), low), w_mod.reshape(deep, 3 * width), (f * deep, 0)
    )
    weights, x, cot, cond_all, bias_all, mod_all = gather(
        mesh, packed, latents_in.astype(low), cotangent.astype(low), cond_rows, biases, mod_padded
    )
    x = x.reshape(C * half, width).astype(full)
    cot = cot.reshape(C * half, width).astype(full)
    weights = weights.reshape(3, width, T * hidden)
    qkvo_full, up_full, down_t = weights[0], weights[1], weights[2]
    outs_t = qkvo_full.reshape(width, T, 4 * part)[:, :, 3 * part :].reshape(width, width)

    bias_all = bias_all.reshape(T, F, -1)
    edges = [3 * deep, b_qv.size, b_out.size, up_projection_bias.size, down_projection_bias.size]
    pieces, start = [], 0
    for size in edges:
        pieces.append(bias_all[:, :, start : start + size])
        start += size
    mod_bias = pieces[0].reshape(T, F, 3, deep).transpose(0, 2, 1, 3).reshape(6, width)
    qv_bias = pieces[1].reshape(T, F, 2, -1).transpose(0, 2, 1, 3).reshape(T, 2, part)
    no_bias = jnp.zeros((T, part), full)
    qkvo_bias = jnp.concatenate([qv_bias[:, 0], no_bias, qv_bias[:, 1], no_bias], axis=1)
    out_bias = pieces[2][0].reshape(width)
    up_bias = pieces[3].reshape(T * hidden)
    down_bias = pieces[4][0].reshape(width)

    modulation = lax.dynamic_index_in_dim(mod_all, own, 1, keepdims=False)
    modulation = modulation.reshape(6, width) + mod_bias
    shift_one, scale_one, gate_one, shift_two, scale_two, gate_two = (
        modulation[k : k + 1] for k in range(6)
    )

    normed_one, inverse_one = normalize(x)
    hidden_one = (normed_one * (1.0 + scale_one) + shift_one).astype(low)
    projected = (dot(hidden_one, qkvo_full) + qkvo_bias.reshape(1, T * hidden)).astype(low)
    attended, log_totals = attention(projected, part)
    branch = dot_bt(attended, outs_t) + out_bias
    middle = x + gate_one * branch
    normed_two, inverse_two = normalize(middle)
    hidden_two = (normed_two * (1.0 + scale_two) + shift_two).astype(low)
    upper_in = dot(hidden_two, up_full) + up_bias
    gelu_value, gelu_pull = jax.vjp(lambda u: jax.nn.gelu(u, approximate=True), upper_in)
    active = gelu_value.astype(low)
    mlp_out = dot_bt(active, down_t) + down_bias
    block_own = (middle + gate_two * mlp_out).astype(low).reshape(C, half, width)

    away = lax.dynamic_index_in_dim(block_own, 1 - c, 0, keepdims=False)
    here = lax.dynamic_index_in_dim(block_own, c, 0, keepdims=False)
    landed = lax.ppermute(away, "ctx", [(0, 1), (1, 0)])

    gate_two_grad = jnp.sum(cot * mlp_out, axis=0)
    down_in = (cot * gate_two).astype(low)
    down_bias_grad = jnp.sum(down_in, axis=0, dtype=full)
    down_grad_t = dot_at(down_in, active)
    upper_grad = gelu_pull(dot(down_in, down_t))[0].astype(low)
    up_bias_grad = jnp.sum(upper_grad, axis=0, dtype=full)
    up_grad = dot_at(hidden_two, upper_grad)
    hidden_two_grad = dot_bt(upper_grad, up_full)
    scale_two_grad = jnp.sum(hidden_two_grad * normed_two, axis=0)
    shift_two_grad = jnp.sum(hidden_two_grad, axis=0)
    middle_grad = cot + norm_back(hidden_two_grad * (1.0 + scale_two), normed_two, inverse_two)
    gate_one_grad = jnp.sum(middle_grad * branch, axis=0)
    branch_grad = (middle_grad * gate_one).astype(low)
    out_bias_grad = jnp.sum(branch_grad, axis=0, dtype=full)
    out_grad_t = dot_at(branch_grad, attended)
    attended_grad = dot(branch_grad, outs_t).astype(low)
    projected_grad = attention_back(projected, attended_grad, log_totals, part)
    all_bias_grad = jnp.sum(projected_grad, axis=0, dtype=full)
    qkvo_grad = dot_at(hidden_one, projected_grad).reshape(width, T, 4 * part)
    qkvo_grad = jnp.concatenate(
        [qkvo_grad[:, :, : 3 * part], out_grad_t.reshape(width, T, part)], axis=2
    ).reshape(width, T * hidden)
    hidden_one_grad = dot_bt(projected_grad, qkvo_full)
    scale_one_grad = jnp.sum(hidden_one_grad * normed_one, axis=0)
    shift_one_grad = jnp.sum(hidden_one_grad, axis=0)
    latents_grad = middle_grad + norm_back(
        hidden_one_grad * (1.0 + scale_one), normed_one, inverse_one
    )
    zeros = jnp.zeros((width,), full)
    mod_grad = jnp.stack(
        [
            shift_one_grad, scale_one_grad, gate_one_grad,
            shift_two_grad, scale_two_grad, gate_two_grad, zeros, zeros,
        ]
    )

    grads = jnp.stack([g.astype(low) for g in (qkvo_grad, up_grad, down_grad_t)])
    grads = grads.reshape(3, F, deep, T * hidden)
    bias_grads = jnp.concatenate(
        [
            all_bias_grad.reshape(T, 4, F, -1)[:, 0:3:2].transpose(0, 2, 1, 3).reshape(T, F, -1),
            up_bias_grad.reshape(T, F, -1),
            jnp.broadcast_to(out_bias_grad.reshape(1, F, deep), (T, F, deep)),
            jnp.broadcast_to(down_bias_grad.reshape(1, F, deep), (T, F, deep)),
        ],
        axis=2,
    )
    count = bias_grads.shape[2]
    bias_grads = jnp.pad(bias_grads, ((0, 0), (0, 0), (0, 1024 * -(-count // 1024) - count)))
    owned, own_bias, latents_grad, block_out, mod_grads, cond_parts = reduce(
        mesh, grads, bias_grads.reshape(T, F, -1, 128), latents_grad.astype(low).reshape(C, half, width),
        here, landed, mod_grad, w_mod.transpose(1, 0, 2),
    )
    owned = owned.astype(full).transpose(1, 2, 0, 3).reshape(3, deep, hidden)
    own_bias = own_bias.reshape(-1)
    qv_size, up_size = b_qv.size, up_projection_bias.size
    qkv_owned = owned[0, :, : 3 * part].reshape(deep, 3, part)
    out_owned = owned[0, :, 3 * part :].T
    up_owned = owned[1]
    down_owned = owned[2].T

    all_mod = mod_grads.transpose(2, 0, 1, 3, 4).reshape(F * group, 8, width)
    own_mod = lax.dynamic_slice_in_dim(all_mod, t * 3, 3, axis=1)
    cond_own = lax.dynamic_slice_in_dim(cond_all[:, :group], f * deep, deep, axis=2)
    mod_weight_grad = jnp.einsum(
        "ld,lkc->dkc", cond_own.reshape(F * group, deep), own_mod,
        precision=lax.Precision.HIGHEST,
    )
    mod_bias_grad = lax.dynamic_slice_in_dim(jnp.sum(own_mod, axis=0), f * deep, deep, axis=1)
    silu_total = cond_parts[:, :group, :deep].transpose(1, 0, 2).reshape(group, width)
    condition_grad = jax.vjp(jax.nn.silu, condition)[1](silu_total)[0]
    return (
        block_out.astype(full),
        latents_grad.astype(full),
        condition_grad,
        mod_weight_grad,
        mod_bias_grad,
        qkv_owned,
        own_bias[:qv_size].reshape(2, -1),
        out_owned,
        own_bias[qv_size + up_size : qv_size + up_size + deep],
        up_owned,
        own_bias[qv_size : qv_size + up_size],
        down_owned,
        own_bias[qv_size + up_size + deep : qv_size + up_size + 2 * deep],
    )


def solution(mesh):
    placed = (
        P("fsdp", "ctx", None),
        P("fsdp", None),
        P("fsdp", "tp", None),
        P("tp", "fsdp"),
        P("fsdp", None, "tp"),
        P(None, ("tp", "fsdp")),
        P("tp", "fsdp"),
        P("fsdp"),
        P("fsdp", "tp"),
        P(("tp", "fsdp")),
        P("tp", "fsdp"),
        P("fsdp"),
        P("fsdp", "ctx", None),
    )
    return jax.shard_map(
        functools.partial(shards, mesh),
        mesh=mesh,
        in_specs=placed,
        out_specs=(
            P("fsdp", "ctx", None),
            P("fsdp", "ctx", None),
            P("fsdp", None),
            P("fsdp", "tp", None),
            P("tp", "fsdp"),
            P("fsdp", None, "tp"),
            P(None, ("tp", "fsdp")),
            P("tp", "fsdp"),
            P("fsdp"),
            P("fsdp", "tp"),
            P(("tp", "fsdp")),
            P("tp", "fsdp"),
            P("fsdp"),
        ),
        check_vma=False,
    )
```
